32 devices in a mesh: parts: 2 (over x), ep: 16 (over z, y, core).
Axes of the slice: x: 2, y: 2, z: 4, core: 2. Of those that a mesh axis runs over, the one named last changes fastest.
Arguments:
- tokens: bfloat16 [3072, 2048], P(('parts', 'ep')), parts along dimension 0, may hold values from -6 to 6
- expert_ids: int32 [3072, 8], P(('parts', 'ep')), parts along dimension 0, may hold values from 0 to 15, as said below
- gate_probs: float32 [3072, 8], P(('parts', 'ep')), parts along dimension 0, may hold values from 0.1 to 1
- lengths: int32 [96], P(('parts', 'ep')), parts along dimension 0, may hold values from 16 to 32, as said below
- block_counts: int32 [32], P('parts'), parts along dimension 0, may hold values from 2 to 6, as said below
- hot_list: int32 [8, 2], P('parts'), parts along dimension 0, may hold values from 0 to 15, as said below
- w_gate: bfloat16 [16, 2048, 768], P('ep'), may hold values from -0.125 to 0.125
- w_up: bfloat16 [16, 2048, 768], P('ep'), may hold values from -0.125 to 0.125
- w_down: bfloat16 [16, 768, 2048], P('ep'), may hold values from -0.21875 to 0.21875
Outputs:
- moe_out: bfloat16 [3072, 2048], P(('parts', 'ep')), parts along dimension 0
The draws below stay inside these ranges and needn't reach their ends.
There are 2 independent parts, one for each index of `parts`. The reference program is written for one: setup_inputs(seed, part) draws one part's arguments, and reference() takes and returns one part's arrays. A program takes and returns all parts, laid end to end along the dimension named above; an argument that names none is the same for every part. Nothing has to cross between parts.
Inputs may be any that keep to these rules, and one draw needn't show every extreme that they name: `expert_ids`: each row names 8 different experts; each expert in column 0 of hot_list is named by exactly 96 rows of every device; no other expert is named by more than 96 rows of one device, and on each device that holds some of the first 192 tokens one unlisted expert is named by exactly 96 rows. `lengths`: every block among the first 192 tokens has 32 live positions; some other block has 16. `block_counts`: every expert in column 0 of hot_list has 6 blocks; every other has 2 to 4 blocks, both ends reached. `hot_list`: column 0 holds 4 different experts; column 1 is column 0 plus half of 16, modulo 16; no expert of column 0 stands in column 1.
All inputs are finite; a program needn't handle non-finite values.
Results may differ from the reference program's by a relative error of at most 0.0058.
Values may be sent and summed in bfloat16 or wider, within the bound.
No kernel may reach another device: no remote copies, remote signals or barrier semaphores. Data moves between devices by JAX's collectives and lax.ppermute only.
A program may use at most 64 MiB of HBM per device.

```python
import math
import jax
import jax.numpy as jnp
from jax import lax

D = 2048
FF = 768
TOP = 8
BLOCK_LEN = 32
BLK = 128
HOT = 4
TOK_DEV = 96
EXPERTS = 16
TOKENS = 1536
SEQS = 48
SLOT = 96
OWN_BLK = 3
REP_BLK = 3
MAXBLK = 6


def listed_experts(key):
    half_axis = EXPERTS // 2
    lower_ids = jax.random.permutation(jax.random.fold_in(key, 11), half_axis)[:HOT]
    upper_flag = jax.random.randint(jax.random.fold_in(key, 12), (HOT,), 0, 2)
    return (lower_ids + half_axis * upper_flag).astype(jnp.int32)


def listed_mask(chosen):
    expert_index = jnp.arange(EXPERTS, dtype=jnp.int32)
    return jnp.sum((expert_index[:, None] == chosen[None, :]).astype(jnp.int32), axis=1) > 0


def cold_ranking(key, chosen):
    expert_index = jnp.arange(EXPERTS, dtype=jnp.int32)
    shuffled = jax.random.permutation(jax.random.fold_in(key, 31), EXPERTS).astype(jnp.int32)
    return jnp.argsort(jnp.where(listed_mask(chosen), EXPERTS + expert_index, shuffled), stable=True).astype(jnp.int32)


def crowded_ranks(key, device):
    return jax.random.permutation(jax.random.fold_in(jax.random.fold_in(key, 41), device), TOK_DEV).astype(jnp.int32)


def all_crowded_ranks(key):
    devices = TOKENS // TOK_DEV
    return jax.vmap(lambda index: crowded_ranks(key, index))(jnp.arange(devices, dtype=jnp.int32))


def draw_tokens(key, part):
    ranks = all_crowded_ranks(key)
    key = jax.random.fold_in(key, 17)
    devices = TOKENS // TOK_DEV
    blank_count = max(1, SLOT // 8)
    device_index = jnp.arange(devices, dtype=jnp.int32)[:, None]
    blank = ((device_index < devices // 8) & (ranks < blank_count)).reshape(TOKENS)
    values = jnp.clip(jax.random.normal(jax.random.fold_in(key, 1), (TOKENS, D), jnp.float32), -6.0, 6.0)
    return jnp.where(blank[:, None], 0.0, values).astype(jnp.bfloat16)


def draw_lengths(key, part):
    key = jax.random.fold_in(key, 13)
    devices = TOKENS // TOK_DEV
    full_blocks = devices // 8 * (TOK_DEV // BLOCK_LEN)
    block_index = jnp.arange(SEQS, dtype=jnp.int32)
    drawn = jax.random.randint(jax.random.fold_in(key, 1), (SEQS,), BLOCK_LEN // 2, BLOCK_LEN + 1)
    short_block = jax.random.randint(jax.random.fold_in(key, 2), (), full_blocks, SEQS)
    drawn = jnp.where(block_index == short_block, BLOCK_LEN // 2, drawn)
    drawn = jnp.where(block_index < full_blocks, BLOCK_LEN, drawn)
    return drawn.astype(jnp.int32)


def draw_hot_list(key, part):
    chosen = listed_experts(key)
    destination = (chosen + EXPERTS // 2) % EXPERTS
    return jnp.stack([chosen, destination], axis=1).astype(jnp.int32)


def draw_block_counts(key, part):
    chosen = listed_experts(key)
    ranking = cold_ranking(key, chosen)
    key = jax.random.fold_in(key, 5)
    expert_index = jnp.arange(EXPERTS, dtype=jnp.int32)
    is_hot = listed_mask(chosen)
    counts = jax.random.randint(key, (EXPERTS,), OWN_BLK - 1, OWN_BLK + 2)
    counts = jnp.where(expert_index == ranking[0], OWN_BLK - 1, counts)
    counts = jnp.where(expert_index == ranking[1], OWN_BLK + 1, counts)
    counts = jnp.where(is_hot, MAXBLK, counts)
    return counts.astype(jnp.int32)


def draw_expert_ids(key, part):
    chosen = listed_experts(key)
    crowded = cold_ranking(key, chosen)[0]
    ranks = all_crowded_ranks(key)
    key = jax.random.fold_in(key, 9)
    devices = TOKENS // TOK_DEV
    expert_index = jnp.arange(EXPERTS, dtype=jnp.int32)
    is_hot = listed_mask(chosen)
    cold_count = EXPERTS - HOT

    def one_device(device_key, device, crowd_rank):
        is_full = device < devices // 8
        excluded = is_hot | is_full & (expert_index == crowded)
        shuffled = jax.random.permutation(jax.random.fold_in(device_key, 1), EXPERTS).astype(jnp.int32)
        cold_order = jnp.argsort(jnp.where(excluded, EXPERTS + expert_index, shuffled), stable=True)[:cold_count]
        cycle_count = cold_count - is_full.astype(jnp.int32)
        extra = jax.random.randint(jax.random.fold_in(device_key, 2), (), TOP, cycle_count + 1)
        row_key = jax.random.fold_in(device_key, 3)

        def hot_rows(column):
            order = jax.random.permutation(jax.random.fold_in(row_key, column), TOK_DEV)
            return order < SLOT
        selected = jax.vmap(hot_rows)(jnp.arange(HOT, dtype=jnp.int32))
        hot_part = jnp.where(selected.T, chosen[None, :], -1)
        crowd_column = jnp.where(is_full & (crowd_rank < SLOT), crowded, -1).astype(jnp.int32)
        grid = jnp.concatenate([hot_part, crowd_column[:, None], jnp.full((TOK_DEV, TOP - HOT - 1), -1, jnp.int32)], axis=1)
        is_cold = grid < 0
        flat_cold = is_cold.reshape(TOK_DEV * TOP).astype(jnp.int32)
        order = jnp.cumsum(flat_cold) - flat_cold
        place = order % (cycle_count + extra)
        place = jnp.where(place < cycle_count, place, place - cycle_count)
        cold_ids = cold_order[place].reshape(TOK_DEV, TOP)
        grid = jnp.where(is_cold, cold_ids, grid)
        shift = jax.random.randint(jax.random.fold_in(device_key, 4), (TOK_DEV, 1), 0, TOP)
        column = (jnp.arange(TOP, dtype=jnp.int32)[None, :] - shift) % TOP
        return jnp.take_along_axis(grid, column, axis=1)
    device_index = jnp.arange(devices, dtype=jnp.int32)
    device_keys = jax.vmap(lambda index: jax.random.fold_in(key, index))(device_index)
    return jax.vmap(one_device)(device_keys, device_index, ranks).reshape(TOKENS, TOP).astype(jnp.int32)


def shard_levels(rng, extent, cuts, low, top_value):
    gain = 1.0
    for dim, blocks in cuts:
        steps = jax.random.uniform(jax.random.fold_in(jax.random.fold_in(rng, 6), dim), (blocks,), jnp.float32, low / len(cuts), top_value / len(cuts))
        gain = gain * jnp.repeat(jnp.exp(steps), extent[dim] // blocks).reshape((-1,) + (1,) * (len(extent) - 1 - dim))
    return gain


def noise(own_key, dims, deviation, limit, split=(), held_as=jnp.bfloat16):
    array = deviation * jax.random.normal(own_key, dims, jnp.float32)
    if split:
        array = array * shard_levels(own_key, dims, split, -0.22, 0.18)
    return jnp.clip(array, -limit, limit).astype(held_as)


def setup_inputs(seed: int = 0, part: int = 0) -> dict:
    keys = jax.random.split(jax.random.key(seed), 10)
    part_splits = jax.random.split(jax.random.fold_in(keys[9], part), 10)
    tokens = draw_tokens(jax.random.fold_in(jax.random.fold_in(keys[9], part), 71), part)
    expert_ids = draw_expert_ids(jax.random.fold_in(jax.random.fold_in(keys[9], part), 71), part)
    gate_probs = jnp.clip(jnp.exp(math.log(1.0) - 2.3025851 * jax.random.uniform(part_splits[2], (TOKENS, TOP), jnp.float32) ** shard_levels(part_splits[2], (TOKENS, TOP), ((0, 16),), -0.2, 0.2)), 0.1, 1.0)
    lengths = draw_lengths(jax.random.fold_in(jax.random.fold_in(keys[9], part), 71), part)
    block_counts = draw_block_counts(jax.random.fold_in(jax.random.fold_in(keys[9], part), 71), part)
    hot_list = draw_hot_list(jax.random.fold_in(jax.random.fold_in(keys[9], part), 71), part)
    w_gate = noise(keys[6], (EXPERTS, D, FF), D ** -0.5, 0.125, ((0, 16),))
    w_up = noise(keys[7], (EXPERTS, D, FF), D ** -0.5, 0.125, ((0, 16),))
    w_down = noise(keys[8], (EXPERTS, FF, D), FF ** -0.5, 0.21875, ((0, 16),))
    return {"tokens": tokens, "expert_ids": expert_ids, "gate_probs": gate_probs, "lengths": lengths, "block_counts": block_counts, "hot_list": hot_list, "w_gate": w_gate, "w_up": w_up, "w_down": w_down}


def expert_forward(gathered, w_gate_e, w_up_e, w_down_e):
    gate = jnp.dot(gathered, w_gate_e, preferred_element_type=jnp.float32)
    up_val = jnp.dot(gathered, w_up_e, preferred_element_type=jnp.float32)
    activation = (jax.nn.silu(gate) * up_val).astype(jnp.bfloat16)
    return jnp.dot(activation, w_down_e, preferred_element_type=jnp.float32).astype(jnp.bfloat16)


def reference(tokens, expert_ids, gate_probs, lengths, block_counts, hot_list, w_gate, w_up, w_down):
    assigned = TOKENS * TOP
    position = jnp.arange(TOKENS, dtype=jnp.int32)
    is_valid = (position % BLOCK_LEN) < jnp.repeat(lengths, BLOCK_LEN)
    flat_ids = expert_ids.reshape(assigned).astype(jnp.int32)
    flat_valid = jnp.repeat(is_valid, TOP)
    experts = jnp.arange(EXPERTS, dtype=jnp.int32)
    onehot = ((flat_ids[:, None] == experts[None, :]) & flat_valid[:, None]).astype(jnp.int32)
    expert_rank = jnp.sum((jnp.cumsum(onehot, axis=0) - onehot) * onehot, axis=1).astype(jnp.int32)
    is_hot = jnp.sum((hot_list[:, 0][None, :] == experts[:, None]).astype(jnp.int32), axis=1).astype(jnp.int32)
    cap_blocks = (block_counts + REP_BLK * is_hot).astype(jnp.int32)
    capacity = BLK * cap_blocks
    is_kept = flat_valid & (expert_rank < capacity[flat_ids])
    block_end = jnp.cumsum(cap_blocks).astype(jnp.int32)
    block_start = block_end - cap_blocks
    total_blocks = (EXPERTS - HOT) * (OWN_BLK + 1) + HOT * (MAXBLK + REP_BLK)
    slot_count = total_blocks * BLK
    target = jnp.where(is_kept, block_start[flat_ids] * BLK + expert_rank, slot_count).astype(jnp.int32)
    slot_table = jnp.full((slot_count,), assigned, jnp.int32)
    slot_table = slot_table.at[target].set(jnp.arange(assigned, dtype=jnp.int32), mode="drop")
    slot_table = slot_table.reshape(total_blocks, BLK)
    block_index = jnp.arange(total_blocks, dtype=jnp.int32)
    block_owner = jnp.sum((block_end[None, :] <= block_index[:, None]).astype(jnp.int32), axis=1)
    block_owner = jnp.minimum(block_owner, EXPERTS - 1).astype(jnp.int32)
    padded = jnp.concatenate([tokens, jnp.zeros((1, D), tokens.dtype)], axis=0)

    def one_block(inputs):
        buffer_slots, owner = inputs
        gathered = padded[buffer_slots // TOP]
        gate_w = lax.dynamic_index_in_dim(w_gate, owner, 0, keepdims=False)
        up_w = lax.dynamic_index_in_dim(w_up, owner, 0, keepdims=False)
        down_w = lax.dynamic_index_in_dim(w_down, owner, 0, keepdims=False)
        return expert_forward(gathered, gate_w, up_w, down_w)

    results = lax.map(one_block, (slot_table, block_owner))
    flat_results = results.reshape(slot_count, D)
    picked = flat_results[jnp.minimum(target, slot_count - 1)].reshape(TOKENS, TOP, D)
    weights = jnp.where(is_kept.reshape(TOKENS, TOP), gate_probs, 0.0)
    mixed_sum = jnp.zeros((TOKENS, D), jnp.float32)
    for column in range(TOP):
        mixed_sum = mixed_sum + weights[:, column, None] * picked[:, column, :].astype(jnp.float32)
    return mixed_sum.astype(jnp.bfloat16)
```

```python
import jax
import jax.numpy as jnp
from jax import lax
from jax.sharding import PartitionSpec as P

BLOCK_LEN = 32
BLK = 128


def expert_forward(gathered, w_gate_e, w_up_e, w_down_e):
    gate = jnp.dot(gathered, w_gate_e, preferred_element_type=jnp.float32)
    up_val = jnp.dot(gathered, w_up_e, preferred_element_type=jnp.float32)
    activation = (jax.nn.silu(gate) * up_val).astype(jnp.bfloat16)
    return jnp.dot(activation, w_down_e, preferred_element_type=jnp.float32).astype(jnp.bfloat16)


def plan_sizes(devices, tok_rows, fan_out, listed):
    assigned = tok_rows * fan_out
    slot_rows = min(2 * assigned // devices, tok_rows)
    cold_load = 3 * devices * (assigned - listed * slot_rows) // (4 * (devices - listed))
    own_blocks = (cold_load + BLK - 1) // BLK
    hot_load = 3 * devices * slot_rows // 4
    spare_blocks = ((hot_load + BLK - 1) // BLK - own_blocks) // 2
    return (slot_rows, own_blocks + spare_blocks, spare_blocks)


def run_blocks(buffer, gate_w, up_w, down_w):
    return expert_forward(buffer, gate_w, up_w, down_w)


def sparse_layer(
    tokens, expert_ids, gate_probs, lengths, block_counts, hot_list, w_gate, w_up, w_down
):
    devices = lax.axis_size("ep")
    my_index = lax.axis_index("ep")
    tok_rows, model_width = tokens.shape
    fan_out = expert_ids.shape[1]
    assigned = tok_rows * fan_out
    slot_rows, most_blocks, spare_blocks = plan_sizes(devices, tok_rows, fan_out, hot_list.shape[0])
    position = jnp.arange(tok_rows, dtype=jnp.int32)
    is_valid = position % BLOCK_LEN < jnp.repeat(lengths, BLOCK_LEN)
    flat_ids = expert_ids.reshape(assigned)
    flat_valid = jnp.repeat(is_valid, fan_out)
    experts = jnp.arange(devices, dtype=jnp.int32)
    onehot = ((flat_ids[:, None] == experts[None, :]) & flat_valid[:, None]).astype(jnp.int32)
    local_rank = jnp.sum((jnp.cumsum(onehot, axis=0) - onehot) * onehot, axis=1)
    counts = jnp.sum(onehot, axis=0)
    all_counts = lax.all_gather(counts[None, :], "ep", axis=0, tiled=True)
    prefix = jnp.cumsum(all_counts, axis=0) - all_counts
    is_hot = jnp.sum((hot_list[:, 0][None, :] == experts[:, None]).astype(jnp.int32), axis=1)
    own_cap = BLK * block_counts
    spare_cap = spare_blocks * BLK * is_hot
    slot_place = jnp.where(flat_valid, flat_ids * slot_rows + local_rank, devices * slot_rows)
    slot_table = jnp.full((devices * slot_rows,), assigned, jnp.int32)
    slot_table = slot_table.at[slot_place].set(jnp.arange(assigned, dtype=jnp.int32), mode="drop")
    padded = jnp.concatenate([tokens, jnp.zeros((1, model_width), tokens.dtype)], axis=0)
    outgoing = padded[slot_table // fan_out].reshape(devices, slot_rows, model_width)
    incoming = lax.all_to_all(outgoing, "ep", split_axis=0, concat_axis=0, tiled=True).reshape(
        devices * slot_rows, model_width
    )
    incoming_pad = jnp.concatenate([incoming, jnp.zeros((1, model_width), incoming.dtype)], axis=0)
    all_slots = devices * slot_rows
    from_counts = lax.dynamic_index_in_dim(all_counts, my_index, 1, keepdims=False)
    from_prefix = lax.dynamic_index_in_dim(prefix, my_index, 1, keepdims=False)
    slot_index = jnp.arange(slot_rows, dtype=jnp.int32)
    global_rank = (from_prefix[:, None] + slot_index[None, :]).reshape(all_slots)
    is_live = (slot_index[None, :] < from_counts[:, None]).reshape(all_slots)
    my_own = lax.dynamic_index_in_dim(own_cap, my_index, 0, keepdims=False)
    my_spare = lax.dynamic_index_in_dim(spare_cap, my_index, 0, keepdims=False)
    rank_limit = my_own + my_spare
    buffer_rows = (most_blocks + spare_blocks) * BLK
    inside = is_live & (global_rank >= 0) & (global_rank < 0 + rank_limit)
    where_to = jnp.where(inside, global_rank - 0, buffer_rows)
    rank_order = jnp.full((buffer_rows,), all_slots, jnp.int32)
    rank_order = rank_order.at[where_to].set(jnp.arange(all_slots, dtype=jnp.int32), mode="drop")
    rows_all = incoming_pad[rank_order]
    results = run_blocks(rows_all, w_gate[0], w_up[0], w_down[0])
    is_kept = is_live & (global_rank < rank_limit)
    result_rows = results.shape[0]
    results_pad = jnp.concatenate([results, jnp.zeros((1, model_width), results.dtype)], axis=0)
    returning = results_pad[jnp.where(is_kept, global_rank, result_rows)].reshape(
        devices, slot_rows, model_width
    )
    returned = lax.all_to_all(returning, "ep", split_axis=0, concat_axis=0, tiled=True).reshape(
        all_slots, model_width
    )
    returned_pad = jnp.concatenate([returned, jnp.zeros((1, model_width), returned.dtype)], axis=0)
    picked = returned_pad[slot_place].reshape(tok_rows, fan_out, model_width)
    weights = jnp.where(is_valid[:, None], gate_probs, 0.0)
    mixed_sum = jnp.zeros((tok_rows, model_width), jnp.float32)
    for column in range(fan_out):
        mixed_sum = mixed_sum + weights[:, column, None] * picked[:, column, :].astype(jnp.float32)
    return mixed_sum.astype(jnp.bfloat16)


def dense_layer(
    tokens, expert_ids, gate_probs, lengths, block_counts, hot_list, w_gate, w_up, w_down
):
    devices = lax.axis_size("ep")
    ring = devices // 4
    me = lax.axis_index("ep")
    tok_rows, width = tokens.shape
    spare_blocks = plan_sizes(devices, tok_rows, expert_ids.shape[1], hot_list.shape[0])[2]

    def ring_pairs(k):
        return [(d, (d + 4 * k) % devices) for d in range(devices)]

    core_pairs = [(d, d ^ 1) for d in range(devices)]
    y_pairs = [(d, d ^ 2) for d in range(devices)]
    over_ring = lambda a, k: lax.ppermute(a, "ep", ring_pairs(k)) if k else a
    over_y = lambda a: lax.ppermute(a, "ep", y_pairs)
    over_core = lambda a: lax.ppermute(a, "ep", core_pairs)

    position = jnp.arange(tok_rows, dtype=jnp.int32)
    is_valid = position % BLOCK_LEN < jnp.repeat(lengths, BLOCK_LEN)
    experts = jnp.arange(devices, dtype=jnp.int32)
    names = (expert_ids[None, :, :] == experts[:, None, None]) & is_valid[None, :, None]
    weight = jnp.sum(jnp.where(names, gate_probs[None], 0.0), axis=2)
    weight = jnp.where(jnp.any(names, axis=2), weight, -1.0)

    order = [0] + sorted(range(1, ring), key=lambda k: min(k, ring - k))
    shards = {k: over_ring(tokens, k) for k in order}
    w_ring = jnp.stack([over_ring(weight, k) for k in range(ring)])
    w_col = jnp.stack([w_ring, over_y(w_ring)], axis=1)
    pick = lambda e: lax.dynamic_index_in_dim(w_col, e, 2, keepdims=False)
    w_mine = jnp.stack([pick(me), over_core(pick(me ^ 1))], axis=1)
    w_mine = w_mine.reshape(ring * 4, tok_rows)
    slot = jnp.arange(devices, dtype=jnp.int32)
    k_of, c_of, y_of = slot // 4, slot // 2 % 2, slot % 2
    source = (me // 4 - k_of) % ring * 4 + ((me // 2 % 2) ^ y_of) * 2 + ((me % 2) ^ c_of)
    live = (w_mine >= 0).astype(jnp.int32)
    counts = jnp.sum(live, axis=1)
    before = jnp.sum(jnp.where(source[None, :] < source[:, None], counts[None, :], 0), axis=1)
    rank = before[:, None] + jnp.cumsum(live, axis=1) - live
    own = lax.dynamic_index_in_dim(block_counts, me, 0, keepdims=False)
    is_hot = jnp.sum((hot_list[:, 0] == me).astype(jnp.int32))
    limit = BLK * (own + spare_blocks * is_hot)
    w_rows = jnp.where((live > 0) & (rank < limit), w_mine, 0.0).reshape(ring, 4 * tok_rows, 1)

    partial = {}
    for k in order:
        pair = jnp.concatenate([shards[k], over_y(shards[k])])
        rows = jnp.concatenate([pair, over_core(pair)])
        gate = jnp.dot(rows, w_gate[0], preferred_element_type=jnp.float32)
        up_val = jnp.dot(rows, w_up[0], preferred_element_type=jnp.float32)
        activation = (jax.nn.silu(gate) * up_val).astype(jnp.bfloat16)
        result = jnp.dot(activation, w_down[0], preferred_element_type=jnp.float32)
        partial[k] = (result * w_rows[k]).astype(jnp.bfloat16)

    f32 = lambda a: a.astype(jnp.float32)
    total = None
    for k in reversed(order):
        mine, theirs = partial[k][: 2 * tok_rows], partial[k][2 * tok_rows :]
        pair = (f32(mine) + f32(over_core(theirs))).astype(jnp.bfloat16)
        block = f32(pair[:tok_rows]) + f32(over_y(pair[tok_rows:]))
        got = f32(over_ring(block.astype(jnp.bfloat16), ring - k)) if k else block
        total = got if total is None else total + got
    return total.astype(jnp.bfloat16)


def per_device(tokens, expert_ids, gate_probs, lengths, block_counts, hot_list, *weights):
    devices = lax.axis_size("ep")
    slot_rows = plan_sizes(devices, tokens.shape[0], expert_ids.shape[1], hot_list.shape[0])[0]
    layer = dense_layer if slot_rows == tokens.shape[0] and devices % 4 == 0 else sparse_layer
    return layer(tokens, expert_ids, gate_probs, lengths, block_counts, hot_list, *weights)


def solution(mesh):
    placed = (
        P(("parts", "ep"), None),
        P(("parts", "ep"), None),
        P(("parts", "ep"), None),
        P(("parts", "ep")),
        P("parts"),
        P("parts", None),
        P("ep", None, None),
        P("ep", None, None),
        P("ep", None, None),
    )
    return jax.shard_map(
        per_device, mesh=mesh, in_specs=placed, out_specs=P(("parts", "ep"), None), check_vma=False
    )
```

```python
import functools

import jax
import jax.numpy as jnp
from jax import lax
from jax.experimental import pallas as pl
from jax.experimental.pallas import tpu as pltpu
from jax.sharding import PartitionSpec as P

BLOCK_LEN = 32
BLK = 128


def expert_forward(gathered, w_gate_e, w_up_e, w_down_e):
    gate = jnp.dot(gathered, w_gate_e, preferred_element_type=jnp.float32)
    up_val = jnp.dot(gathered, w_up_e, preferred_element_type=jnp.float32)
    activation = (jax.nn.silu(gate) * up_val).astype(jnp.bfloat16)
    return jnp.dot(activation, w_down_e, preferred_element_type=jnp.float32).astype(jnp.bfloat16)


def plan_sizes(devices, tok_rows, fan_out, listed):
    assigned = tok_rows * fan_out
    slot_rows = min(2 * assigned // devices, tok_rows)
    cold_load = 3 * devices * (assigned - listed * slot_rows) // (4 * (devices - listed))
    own_blocks = (cold_load + BLK - 1) // BLK
    hot_load = 3 * devices * slot_rows // 4
    spare_blocks = ((hot_load + BLK - 1) // BLK - own_blocks) // 2
    return (slot_rows, own_blocks + spare_blocks, spare_blocks)


def run_blocks(buffer, gate_w, up_w, down_w):
    return expert_forward(buffer, gate_w, up_w, down_w)


def sparse_layer(
    tokens, expert_ids, gate_probs, lengths, block_counts, hot_list, w_gate, w_up, w_down
):
    devices = lax.axis_size("ep")
    my_index = lax.axis_index("ep")
    tok_rows, model_width = tokens.shape
    fan_out = expert_ids.shape[1]
    assigned = tok_rows * fan_out
    slot_rows, most_blocks, spare_blocks = plan_sizes(devices, tok_rows, fan_out, hot_list.shape[0])
    position = jnp.arange(tok_rows, dtype=jnp.int32)
    is_valid = position % BLOCK_LEN < jnp.repeat(lengths, BLOCK_LEN)
    flat_ids = expert_ids.reshape(assigned)
    flat_valid = jnp.repeat(is_valid, fan_out)
    experts = jnp.arange(devices, dtype=jnp.int32)
    onehot = ((flat_ids[:, None] == experts[None, :]) & flat_valid[:, None]).astype(jnp.int32)
    local_rank = jnp.sum((jnp.cumsum(onehot, axis=0) - onehot) * onehot, axis=1)
    counts = jnp.sum(onehot, axis=0)
    all_counts = lax.all_gather(counts[None, :], "ep", axis=0, tiled=True)
    prefix = jnp.cumsum(all_counts, axis=0) - all_counts
    is_hot = jnp.sum((hot_list[:, 0][None, :] == experts[:, None]).astype(jnp.int32), axis=1)
    own_cap = BLK * block_counts
    spare_cap = spare_blocks * BLK * is_hot
    slot_place = jnp.where(flat_valid, flat_ids * slot_rows + local_rank, devices * slot_rows)
    slot_table = jnp.full((devices * slot_rows,), assigned, jnp.int32)
    slot_table = slot_table.at[slot_place].set(jnp.arange(assigned, dtype=jnp.int32), mode="drop")
    padded = jnp.concatenate([tokens, jnp.zeros((1, model_width), tokens.dtype)], axis=0)
    outgoing = padded[slot_table // fan_out].reshape(devices, slot_rows, model_width)
    incoming = lax.all_to_all(outgoing, "ep", split_axis=0, concat_axis=0, tiled=True).reshape(
        devices * slot_rows, model_width
    )
    incoming_pad = jnp.concatenate([incoming, jnp.zeros((1, model_width), incoming.dtype)], axis=0)
    all_slots = devices * slot_rows
    from_counts = lax.dynamic_index_in_dim(all_counts, my_index, 1, keepdims=False)
    from_prefix = lax.dynamic_index_in_dim(prefix, my_index, 1, keepdims=False)
    slot_index = jnp.arange(slot_rows, dtype=jnp.int32)
    global_rank = (from_prefix[:, None] + slot_index[None, :]).reshape(all_slots)
    is_live = (slot_index[None, :] < from_counts[:, None]).reshape(all_slots)
    my_own = lax.dynamic_index_in_dim(own_cap, my_index, 0, keepdims=False)
    my_spare = lax.dynamic_index_in_dim(spare_cap, my_index, 0, keepdims=False)
    rank_limit = my_own + my_spare
    buffer_rows = (most_blocks + spare_blocks) * BLK
    inside = is_live & (global_rank >= 0) & (global_rank < 0 + rank_limit)
    where_to = jnp.where(inside, global_rank - 0, buffer_rows)
    rank_order = jnp.full((buffer_rows,), all_slots, jnp.int32)
    rank_order = rank_order.at[where_to].set(jnp.arange(all_slots, dtype=jnp.int32), mode="drop")
    rows_all = incoming_pad[rank_order]
    results = run_blocks(rows_all, w_gate[0], w_up[0], w_down[0])
    is_kept = is_live & (global_rank < rank_limit)
    result_rows = results.shape[0]
    results_pad = jnp.concatenate([results, jnp.zeros((1, model_width), results.dtype)], axis=0)
    returning = results_pad[jnp.where(is_kept, global_rank, result_rows)].reshape(
        devices, slot_rows, model_width
    )
    returned = lax.all_to_all(returning, "ep", split_axis=0, concat_axis=0, tiled=True).reshape(
        all_slots, model_width
    )
    returned_pad = jnp.concatenate([returned, jnp.zeros((1, model_width), returned.dtype)], axis=0)
    picked = returned_pad[slot_place].reshape(tok_rows, fan_out, model_width)
    weights = jnp.where(is_valid[:, None], gate_probs, 0.0)
    mixed_sum = jnp.zeros((tok_rows, model_width), jnp.float32)
    for column in range(fan_out):
        mixed_sum = mixed_sum + weights[:, column, None] * picked[:, column, :].astype(jnp.float32)
    return mixed_sum.astype(jnp.bfloat16)


def weight_kernel(lengths, ids_ref, probs_ref, out, ids, probs, sems):
    copies = [
        pltpu.make_async_copy(ids_ref, ids, sems.at[0]),
        pltpu.make_async_copy(probs_ref, probs, sems.at[1]),
    ]
    for copy in copies:
        copy.start()
    for copy in copies:
        copy.wait()
    fan_out, rows = ids.shape
    experts, lanes = out.shape
    token = lax.broadcasted_iota(jnp.int32, (experts, rows), 1)
    expert = lax.broadcasted_iota(jnp.int32, (experts, rows), 0)
    live_len = jnp.zeros((experts, rows), jnp.int32)
    for block in range(lengths.shape[0]):
        live_len = jnp.where(token // BLOCK_LEN == block, lengths[block], live_len)
    is_valid = token % BLOCK_LEN < live_len
    weight = jnp.full((experts, rows), -1.0, jnp.float32)
    for k in range(fan_out):
        weight = jnp.where(is_valid & (ids[k : k + 1, :] == expert), probs[k : k + 1, :], weight)
    out[...] = jnp.full((experts, lanes), -1.0, jnp.float32)
    out[:, :rows] = weight


def load_kernel(*refs):
    half = len(refs) // 2
    copies = [
        pltpu.make_async_copy(refs[i], refs[half + i], refs[-1].at[i]) for i in range(half)
    ]
    for copy in copies:
        copy.start()
    for copy in copies:
        copy.wait()


def column_kernel(w0, w1, w2, w3, *outs):
    me = lax.axis_index("ep")
    ring = len(outs)
    for k, out in enumerate(outs):
        expert = (me // 4 + k) % ring * 4 + me % 4
        for row, ref in enumerate((w0, w1, w2, w3)):
            out[row : row + 1, :] = ref[pl.ds(expert, 1), :]


def rank_kernel(spare_blocks, block_counts, hot_list, *refs):
    columns, out, held = refs[:-2], refs[-2], refs[-1]
    me = lax.axis_index("ep")
    ring = len(columns)
    slots, lanes = out.shape
    for k, ref in enumerate(columns):
        held[4 * k : 4 * k + 4, :] = ref[:4, :]
    weight = held[...]
    live = weight >= 0.0
    ones = live.astype(jnp.float32)
    first = lax.broadcasted_iota(jnp.int32, (lanes, lanes), 0)
    second = lax.broadcasted_iota(jnp.int32, (lanes, lanes), 1)
    earlier = (first < second).astype(jnp.bfloat16)
    rank = jnp.dot(ones.astype(jnp.bfloat16), earlier, preferred_element_type=jnp.float32)
    counts = jnp.sum(ones, axis=1, keepdims=True)

    def source(slot):
        k, core, y = slot // 4, slot // 2 % 2, slot % 2
        return (me // 4 - k + ring) % ring * 4 + (me // 2 + y) % 2 * 2 + (me + core) % 2

    place = source(lax.broadcasted_iota(jnp.int32, (slots, 1), 0))
    before = jnp.zeros((slots, 1), jnp.float32)
    for slot in range(slots):
        before = before + jnp.where(source(slot) < place, counts[slot : slot + 1, :], 0.0)
    limit = block_counts[me]
    for row in range(hot_list.shape[1]):
        limit = limit + jnp.where(hot_list[0, row] == me, spare_blocks, 0)
    kept = live & (rank + before < (limit * BLK).astype(jnp.float32))
    out[...] = jnp.where(kept, weight, 0.0)


def expert_kernel(slot, a, b, c, d, weight, w_gate, w_up, w_down, o_a, o_b, o_cd, *scratch):
    x, act, res, in_sem, out_sem = scratch
    rows, width = a.shape
    hidden = act.shape[1]
    tile, out_tile = min(256, hidden), width // (out_sem.shape[0] // 3)
    copies = [
        pltpu.make_async_copy(src, x.at[pl.ds(i * rows, rows)], in_sem.at[i])
        for i, src in enumerate((a, b, c, d))
    ]
    for copy in copies:
        copy.start()
    row = lax.broadcasted_iota(jnp.int32, (rows, weight.shape[1]), 0)
    lane = lax.broadcasted_iota(jnp.int32, (rows, weight.shape[1]), 1)
    scale = jnp.concatenate(
        [
            jnp.sum(jnp.where(row == lane, weight[4 * slot + i : 4 * slot + i + 1, :], 0.0), axis=1, keepdims=True)
            for i in range(4)
        ],
        axis=0,
    )
    for copy in copies:
        copy.wait()
    for j in range(hidden // tile):
        part = slice(j * tile, (j + 1) * tile)
        gate = jnp.dot(x[...], w_gate[:, part], preferred_element_type=jnp.float32)
        up_val = jnp.dot(x[...], w_up[:, part], preferred_element_type=jnp.float32)
        act[:, part] = (gate / (1.0 + jnp.exp(-gate)) * up_val).astype(act.dtype)
    sent = []
    for j in range(width // out_tile):
        part = slice(j * out_tile, (j + 1) * out_tile)
        result = jnp.dot(act[...], w_down[:, part], preferred_element_type=jnp.float32)
        res[:, part] = (result * scale).astype(res.dtype)
        at = pl.ds(j * out_tile, out_tile)
        for i, (out, start) in enumerate(((o_cd, 2), (o_b, 1), (o_a, 0))):
            src = res.at[pl.ds(start * rows, out.shape[0]), at]
            sent.append(pltpu.make_async_copy(src, out.at[:, at], out_sem.at[3 * j + i]))
            sent[-1].start()
    for copy in sent:
        copy.wait()


def expert_rows(slot, pieces, weight, matrices):
    rows, width = pieces[0].shape
    hidden = matrices[0].shape[1]
    dtype = pieces[0].dtype
    anywhere = pl.BlockSpec(memory_space=pl.ANY)
    vmem = pl.BlockSpec(memory_space=pltpu.VMEM)
    out_steps = 4
    matrices = [pltpu.with_memory_space_constraint(m, pltpu.VMEM) for m in matrices]
    return pl.pallas_call(
        functools.partial(expert_kernel, slot),
        in_specs=[anywhere] * 4 + [vmem] * 4,
        out_specs=[anywhere] * 3,
        out_shape=[
            jax.ShapeDtypeStruct((rows, width), dtype),
            jax.ShapeDtypeStruct((rows, width), dtype),
            jax.ShapeDtypeStruct((2 * rows, width), dtype),
        ],
        scratch_shapes=[
            pltpu.VMEM((4 * rows, width), dtype),
            pltpu.VMEM((4 * rows, hidden), dtype),
            pltpu.VMEM((4 * rows, width), dtype),
            pltpu.SemaphoreType.DMA((4,)),
            pltpu.SemaphoreType.DMA((3 * out_steps,)),
        ],
        compiler_params=pltpu.CompilerParams(vmem_limit_bytes=20 * 1024 * 1024),
        cost_estimate=pl.CostEstimate(
            flops=24 * rows * width * hidden,
            bytes_accessed=6 * width * hidden + 16 * rows * width,
            transcendentals=4 * rows * hidden,
        ),
        name="expert",
    )(*pieces, weight, *matrices)


def dense_layer(
    tokens, expert_ids, gate_probs, lengths, block_counts, hot_list, w_gate, w_up, w_down
):
    devices = lax.axis_size("ep")
    ring = devices // 4
    tok_rows = tokens.shape[0]
    lanes = (tok_rows + 127) // 128 * 128
    spare_blocks = plan_sizes(devices, tok_rows, expert_ids.shape[1], hot_list.shape[0])[2]

    def ring_pairs(k):
        return [(d, (d + 4 * k) % devices) for d in range(devices)]

    core_pairs = [(d, d ^ 1) for d in range(devices)]
    y_pairs = [(d, d ^ 2) for d in range(devices)]
    over_ring = lambda a, k: lax.ppermute(a, "ep", ring_pairs(k)) if k else a
    over_y = lambda a: lax.ppermute(a, "ep", y_pairs)
    over_core = lambda a: lax.ppermute(a, "ep", core_pairs)
    after = lambda value, *others: lax.optimization_barrier((value,) + others)[0]
    f32 = lambda v: v.astype(jnp.float32)
    bf16 = lambda v: v.astype(jnp.bfloat16)
    vmem = pl.BlockSpec(memory_space=pltpu.VMEM)
    smem = pl.BlockSpec(memory_space=pltpu.SMEM)
    anywhere = pl.BlockSpec(memory_space=pl.ANY)
    hbm = lambda v: pltpu.with_memory_space_constraint(v, pltpu.HBM)
    small = pltpu.CompilerParams(vmem_limit_bytes=2 * 1024 * 1024)

    matrices = [hbm(m[0]) for m in (w_gate, w_up, w_down)]
    matrices = pl.pallas_call(
        load_kernel,
        in_specs=[anywhere] * 3,
        out_specs=[vmem] * 3,
        out_shape=[pltpu.VMEM(m.shape, m.dtype) for m in matrices],
        scratch_shapes=[pltpu.SemaphoreType.DMA((3,))],
        compiler_params=small,
        name="load",
    )(*matrices)
    own_w = pl.pallas_call(
        weight_kernel,
        in_specs=[smem, anywhere, anywhere],
        out_specs=vmem,
        out_shape=jax.ShapeDtypeStruct((devices, lanes), jnp.float32),
        scratch_shapes=[
            pltpu.VMEM(expert_ids.shape[::-1], jnp.int32),
            pltpu.VMEM(gate_probs.shape[::-1], jnp.float32),
            pltpu.SemaphoreType.DMA((2,)),
        ],
        compiler_params=small,
        name="weights",
    )(lengths, hbm(expert_ids.T), hbm(gate_probs.T))
    sent = after(tokens, own_w)
    y_w = over_y(own_w)
    columns = pl.pallas_call(
        column_kernel,
        in_specs=[vmem] * 4,
        out_specs=[vmem] * ring,
        out_shape=[jax.ShapeDtypeStruct((8, lanes), jnp.float32)] * ring,
        compiler_params=small,
        name="columns",
    )(after(own_w, matrices[0]), y_w, over_core(own_w), over_core(y_w))
    s1, s3 = over_ring(sent, 1), over_ring(sent, 3)
    s1 = after(s1, columns[0])
    columns = [over_ring(column, k) for k, column in enumerate(columns)]
    s3 = after(s3, *columns[1:])
    s2 = over_ring(s1, 1)
    weight = pl.pallas_call(
        functools.partial(rank_kernel, spare_blocks),
        in_specs=[smem, smem] + [vmem] * ring,
        out_specs=vmem,
        out_shape=jax.ShapeDtypeStruct((devices, lanes), jnp.float32),
        scratch_shapes=[pltpu.VMEM((devices, lanes), jnp.float32)],
        compiler_params=small,
        name="ranks",
    )(block_counts, hot_list.T, *columns)

    def expert(k, *pieces):
        return expert_rows(k, pieces, weight, matrices)

    def merge_core(a, b, cd):
        cd = over_core(cd)
        return f32(a) + f32(cd[:tok_rows]), bf16(f32(b) + f32(cd[tok_rows:]))

    y_own = over_y(sent)
    y1, y3 = over_y(s1), over_y(s3)
    p0 = expert(0, tokens, y_own, over_core(sent), over_core(y_own))
    y1 = after(y1, p0[0])
    p1 = expert(1, s1, y1, over_core(s1), over_core(y1))
    y3 = after(y3, p1[0])
    p3 = expert(3, s3, y3, over_core(s3), over_core(y3))
    y2 = after(over_y(s2), p3[0])
    a1, b1 = merge_core(*p1)
    p2 = expert(2, after(s2, b1), y2, over_core(s2), over_core(y2))

    (a2, b2), (a3, b3), (a0, b0) = merge_core(*p2), merge_core(*p3), merge_core(*p0)
    block1 = after(a1, b2) + f32(over_y(b1))
    block2 = bf16(a2 + f32(over_y(b2)))
    hop = over_ring(block2, ring - 1)
    block3 = bf16(a3 + f32(over_y(after(b3, b2))))
    block0 = a0 + f32(over_y(after(b0, block2)))
    hop = over_ring(bf16(block1 + f32(hop)), ring - 1)
    return bf16(block0 + f32(over_ring(block3, 1)) + f32(hop))


def per_device(tokens, expert_ids, gate_probs, lengths, block_counts, hot_list, *weights):
    devices = lax.axis_size("ep")
    slot_rows = plan_sizes(devices, tokens.shape[0], expert_ids.shape[1], hot_list.shape[0])[0]
    layer = dense_layer if slot_rows == tokens.shape[0] and devices == 16 else sparse_layer
    return layer(tokens, expert_ids, gate_probs, lengths, block_counts, hot_list, *weights)


def solution(mesh):
    placed = (
        P(("parts", "ep"), None),
        P(("parts", "ep"), None),
        P(("parts", "ep"), None),
        P(("parts", "ep")),
        P("parts"),
        P("parts", None),
        P("ep", None, None),
        P("ep", None, None),
        P("ep", None, None),
    )
    return jax.shard_map(
        per_device, mesh=mesh, in_specs=placed, out_specs=P(("parts", "ep"), None), check_vma=False
    )
```

```python
import functools

import jax
import jax.numpy as jnp
from jax import lax
from jax.experimental import pallas as pl
from jax.experimental.pallas import tpu as pltpu
from jax.sharding import PartitionSpec as P

BLOCK_LEN = 32
BLK = 128


def expert_forward(gathered, w_gate_e, w_up_e, w_down_e):
    gate = jnp.dot(gathered, w_gate_e, preferred_element_type=jnp.float32)
    up_val = jnp.dot(gathered, w_up_e, preferred_element_type=jnp.float32)
    activation = (jax.nn.silu(gate) * up_val).astype(jnp.bfloat16)
    return jnp.dot(activation, w_down_e, preferred_element_type=jnp.float32).astype(jnp.bfloat16)


def plan_sizes(devices, tok_rows, fan_out, listed):
    assigned = tok_rows * fan_out
    slot_rows = min(2 * assigned // devices, tok_rows)
    cold_load = 3 * devices * (assigned - listed * slot_rows) // (4 * (devices - listed))
    own_blocks = (cold_load + BLK - 1) // BLK
    hot_load = 3 * devices * slot_rows // 4
    spare_blocks = ((hot_load + BLK - 1) // BLK - own_blocks) // 2
    return (slot_rows, own_blocks + spare_blocks, spare_blocks)


def run_blocks(buffer, gate_w, up_w, down_w):
    return expert_forward(buffer, gate_w, up_w, down_w)


def sparse_layer(
    tokens, expert_ids, gate_probs, lengths, block_counts, hot_list, w_gate, w_up, w_down
):
    devices = lax.axis_size("ep")
    my_index = lax.axis_index("ep")
    tok_rows, model_width = tokens.shape
    fan_out = expert_ids.shape[1]
    assigned = tok_rows * fan_out
    slot_rows, most_blocks, spare_blocks = plan_sizes(devices, tok_rows, fan_out, hot_list.shape[0])
    position = jnp.arange(tok_rows, dtype=jnp.int32)
    is_valid = position % BLOCK_LEN < jnp.repeat(lengths, BLOCK_LEN)
    flat_ids = expert_ids.reshape(assigned)
    flat_valid = jnp.repeat(is_valid, fan_out)
    experts = jnp.arange(devices, dtype=jnp.int32)
    onehot = ((flat_ids[:, None] == experts[None, :]) & flat_valid[:, None]).astype(jnp.int32)
    local_rank = jnp.sum((jnp.cumsum(onehot, axis=0) - onehot) * onehot, axis=1)
    counts = jnp.sum(onehot, axis=0)
    all_counts = lax.all_gather(counts[None, :], "ep", axis=0, tiled=True)
    prefix = jnp.cumsum(all_counts, axis=0) - all_counts
    is_hot = jnp.sum((hot_list[:, 0][None, :] == experts[:, None]).astype(jnp.int32), axis=1)
    own_cap = BLK * block_counts
    spare_cap = spare_blocks * BLK * is_hot
    slot_place = jnp.where(flat_valid, flat_ids * slot_rows + local_rank, devices * slot_rows)
    slot_table = jnp.full((devices * slot_rows,), assigned, jnp.int32)
    slot_table = slot_table.at[slot_place].set(jnp.arange(assigned, dtype=jnp.int32), mode="drop")
    padded = jnp.concatenate([tokens, jnp.zeros((1, model_width), tokens.dtype)], axis=0)
    outgoing = padded[slot_table // fan_out].reshape(devices, slot_rows, model_width)
    incoming = lax.all_to_all(outgoing, "ep", split_axis=0, concat_axis=0, tiled=True).reshape(
        devices * slot_rows, model_width
    )
    incoming_pad = jnp.concatenate([incoming, jnp.zeros((1, model_width), incoming.dtype)], axis=0)
    all_slots = devices * slot_rows
    from_counts = lax.dynamic_index_in_dim(all_counts, my_index, 1, keepdims=False)
    from_prefix = lax.dynamic_index_in_dim(prefix, my_index, 1, keepdims=False)
    slot_index = jnp.arange(slot_rows, dtype=jnp.int32)
    global_rank = (from_prefix[:, None] + slot_index[None, :]).reshape(all_slots)
    is_live = (slot_index[None, :] < from_counts[:, None]).reshape(all_slots)
    my_own = lax.dynamic_index_in_dim(own_cap, my_index, 0, keepdims=False)
    my_spare = lax.dynamic_index_in_dim(spare_cap, my_index, 0, keepdims=False)
    rank_limit = my_own + my_spare
    buffer_rows = (most_blocks + spare_blocks) * BLK
    inside = is_live & (global_rank >= 0) & (global_rank < 0 + rank_limit)
    where_to = jnp.where(inside, global_rank - 0, buffer_rows)
    rank_order = jnp.full((buffer_rows,), all_slots, jnp.int32)
    rank_order = rank_order.at[where_to].set(jnp.arange(all_slots, dtype=jnp.int32), mode="drop")
    rows_all = incoming_pad[rank_order]
    results = run_blocks(rows_all, w_gate[0], w_up[0], w_down[0])
    is_kept = is_live & (global_rank < rank_limit)
    result_rows = results.shape[0]
    results_pad = jnp.concatenate([results, jnp.zeros((1, model_width), results.dtype)], axis=0)
    returning = results_pad[jnp.where(is_kept, global_rank, result_rows)].reshape(
        devices, slot_rows, model_width
    )
    returned = lax.all_to_all(returning, "ep", split_axis=0, concat_axis=0, tiled=True).reshape(
        all_slots, model_width
    )
    returned_pad = jnp.concatenate([returned, jnp.zeros((1, model_width), returned.dtype)], axis=0)
    picked = returned_pad[slot_place].reshape(tok_rows, fan_out, model_width)
    weights = jnp.where(is_valid[:, None], gate_probs, 0.0)
    mixed_sum = jnp.zeros((tok_rows, model_width), jnp.float32)
    for column in range(fan_out):
        mixed_sum = mixed_sum + weights[:, column, None] * picked[:, column, :].astype(jnp.float32)
    return mixed_sum.astype(jnp.bfloat16)


def weight_kernel(lengths, ids_ref, probs_ref, out, ids, probs, sems):
    copies = [
        pltpu.make_async_copy(ids_ref, ids, sems.at[0]),
        pltpu.make_async_copy(probs_ref, probs, sems.at[1]),
    ]
    for copy in copies:
        copy.start()
    for copy in copies:
        copy.wait()
    fan_out, rows = ids.shape
    experts, lanes = out.shape
    token = lax.broadcasted_iota(jnp.int32, (experts, rows), 1)
    expert = lax.broadcasted_iota(jnp.int32, (experts, rows), 0)
    live_len = jnp.zeros((experts, rows), jnp.int32)
    for block in range(lengths.shape[0]):
        live_len = jnp.where(token // BLOCK_LEN == block, lengths[block], live_len)
    is_valid = token % BLOCK_LEN < live_len
    weight = jnp.full((experts, rows), -1.0, jnp.float32)
    for k in range(fan_out):
        weight = jnp.where(is_valid & (ids[k : k + 1, :] == expert), probs[k : k + 1, :], weight)
    out[...] = jnp.full((experts, lanes), -1.0, jnp.float32)
    out[:, :rows] = weight


def load_kernel(*refs):
    half = len(refs) // 2
    copies = [
        pltpu.make_async_copy(refs[i], refs[half + i], refs[-1].at[i]) for i in range(half)
    ]
    for copy in copies:
        copy.start()
    for copy in copies:
        copy.wait()


def column_kernel(w0, w1, w2, w3, *outs):
    me = lax.axis_index("ep")
    ring = len(outs)
    for k, out in enumerate(outs):
        expert = (me // 4 + k) % ring * 4 + me % 4
        for row, ref in enumerate((w0, w1, w2, w3)):
            out[row : row + 1, :] = ref[pl.ds(expert, 1), :]


def rank_kernel(spare_blocks, block_counts, hot_list, *refs):
    columns, out, held = refs[:-2], refs[-2], refs[-1]
    me = lax.axis_index("ep")
    ring = len(columns)
    slots, lanes = out.shape
    for k, ref in enumerate(columns):
        held[4 * k : 4 * k + 4, :] = ref[:4, :]
    weight = held[...]
    live = weight >= 0.0
    ones = live.astype(jnp.float32)
    first = lax.broadcasted_iota(jnp.int32, (lanes, lanes), 0)
    second = lax.broadcasted_iota(jnp.int32, (lanes, lanes), 1)
    earlier = (first < second).astype(jnp.bfloat16)
    rank = jnp.dot(ones.astype(jnp.bfloat16), earlier, preferred_element_type=jnp.float32)
    counts = jnp.sum(ones, axis=1, keepdims=True)

    def source(slot):
        k, core, y = slot // 4, slot // 2 % 2, slot % 2
        return (me // 4 - k + ring) % ring * 4 + (me // 2 + y) % 2 * 2 + (me + core) % 2

    place = source(lax.broadcasted_iota(jnp.int32, (slots, 1), 0))
    before = jnp.zeros((slots, 1), jnp.float32)
    for slot in range(slots):
        before = before + jnp.where(source(slot) < place, counts[slot : slot + 1, :], 0.0)
    limit = block_counts[me]
    for row in range(hot_list.shape[1]):
        limit = limit + jnp.where(hot_list[0, row] == me, spare_blocks, 0)
    kept = live & (rank + before < (limit * BLK).astype(jnp.float32))
    out[...] = jnp.where(kept, weight, 0.0)


def expert_kernel(slot, a, b, c, d, weight, w_gate, w_up, w_down, o_a, o_b, o_cd, *scratch):
    x, act, res, in_sem, out_sem = scratch
    rows, width = a.shape
    hidden = act.shape[1]
    tile, out_tile = min(256, hidden), width // (out_sem.shape[0] // 3)
    copies = [
        pltpu.make_async_copy(src, x.at[pl.ds(i * rows, rows)], in_sem.at[i])
        for i, src in enumerate((a, b, c, d))
    ]
    for copy in copies:
        copy.start()
    row = lax.broadcasted_iota(jnp.int32, (rows, weight.shape[1]), 0)
    lane = lax.broadcasted_iota(jnp.int32, (rows, weight.shape[1]), 1)
    scale = jnp.concatenate(
        [
            jnp.sum(jnp.where(row == lane, weight[4 * slot + i : 4 * slot + i + 1, :], 0.0), axis=1, keepdims=True)
            for i in range(4)
        ],
        axis=0,
    )
    for copy in copies:
        copy.wait()
    for j in range(hidden // tile):
        part = slice(j * tile, (j + 1) * tile)
        gate = jnp.dot(x[...], w_gate[:, part], preferred_element_type=jnp.float32)
        up_val = jnp.dot(x[...], w_up[:, part], preferred_element_type=jnp.float32)
        act[:, part] = (gate / (1.0 + jnp.exp(-gate)) * up_val).astype(act.dtype)
    sent = []
    for j in range(width // out_tile):
        part = slice(j * out_tile, (j + 1) * out_tile)
        result = jnp.dot(act[...], w_down[:, part], preferred_element_type=jnp.float32)
        res[:, part] = (result * scale).astype(res.dtype)
        at = pl.ds(j * out_tile, out_tile)
        for i, (out, start) in enumerate(((o_cd, 2), (o_b, 1), (o_a, 0))):
            src = res.at[pl.ds(start * rows, out.shape[0]), at]
            sent.append(pltpu.make_async_copy(src, out.at[:, at], out_sem.at[3 * j + i]))
            sent[-1].start()
    for copy in sent:
        copy.wait()


def expert_rows(slot, pieces, weight, matrices):
    rows, width = pieces[0].shape
    hidden = matrices[0].shape[1]
    dtype = pieces[0].dtype
    anywhere = pl.BlockSpec(memory_space=pl.ANY)
    vmem = pl.BlockSpec(memory_space=pltpu.VMEM)
    out_steps = 4
    matrices = [pltpu.with_memory_space_constraint(m, pltpu.VMEM) for m in matrices]
    return pl.pallas_call(
        functools.partial(expert_kernel, slot),
        in_specs=[anywhere] * 4 + [vmem] * 4,
        out_specs=[anywhere] * 3,
        out_shape=[
            jax.ShapeDtypeStruct((rows, width), dtype),
            jax.ShapeDtypeStruct((rows, width), dtype),
            jax.ShapeDtypeStruct((2 * rows, width), dtype),
        ],
        scratch_shapes=[
            pltpu.VMEM((4 * rows, width), dtype),
            pltpu.VMEM((4 * rows, hidden), dtype),
            pltpu.VMEM((4 * rows, width), dtype),
            pltpu.SemaphoreType.DMA((4,)),
            pltpu.SemaphoreType.DMA((3 * out_steps,)),
        ],
        compiler_params=pltpu.CompilerParams(vmem_limit_bytes=20 * 1024 * 1024),
        cost_estimate=pl.CostEstimate(
            flops=24 * rows * width * hidden,
            bytes_accessed=6 * width * hidden + 16 * rows * width,
            transcendentals=4 * rows * hidden,
        ),
        name="expert",
    )(*pieces, weight, *matrices)


def dense_layer(
    tokens, expert_ids, gate_probs, lengths, block_counts, hot_list, w_gate, w_up, w_down
):
    devices = lax.axis_size("ep")
    ring = devices // 4
    tok_rows = tokens.shape[0]
    lanes = (tok_rows + 127) // 128 * 128
    spare_blocks = plan_sizes(devices, tok_rows, expert_ids.shape[1], hot_list.shape[0])[2]

    def ring_pairs(k):
        return [(d, (d + 4 * k) % devices) for d in range(devices)]

    core_pairs = [(d, d ^ 1) for d in range(devices)]
    y_pairs = [(d, d ^ 2) for d in range(devices)]
    over_ring = lambda a, k: lax.ppermute(a, "ep", ring_pairs(k)) if k else a
    over_y = lambda a: lax.ppermute(a, "ep", y_pairs)
    over_core = lambda a: lax.ppermute(a, "ep", core_pairs)
    after = lambda value, *others: lax.optimization_barrier((value,) + others)[0]
    f32 = lambda v: v.astype(jnp.float32)
    bf16 = lambda v: v.astype(jnp.bfloat16)
    vmem = pl.BlockSpec(memory_space=pltpu.VMEM)
    smem = pl.BlockSpec(memory_space=pltpu.SMEM)
    anywhere = pl.BlockSpec(memory_space=pl.ANY)
    hbm = lambda v: pltpu.with_memory_space_constraint(v, pltpu.HBM)
    small = pltpu.CompilerParams(vmem_limit_bytes=2 * 1024 * 1024)

    matrices = [hbm(m[0]) for m in (w_gate, w_up, w_down)]
    matrices = pl.pallas_call(
        load_kernel,
        in_specs=[anywhere] * 3,
        out_specs=[vmem] * 3,
        out_shape=[pltpu.VMEM(m.shape, m.dtype) for m in matrices],
        scratch_shapes=[pltpu.SemaphoreType.DMA((3,))],
        compiler_params=small,
        name="load",
    )(*matrices)
    own_w = pl.pallas_call(
        weight_kernel,
        in_specs=[smem, anywhere, anywhere],
        out_specs=vmem,
        out_shape=jax.ShapeDtypeStruct((devices, lanes), jnp.float32),
        scratch_shapes=[
            pltpu.VMEM(expert_ids.shape[::-1], jnp.int32),
            pltpu.VMEM(gate_probs.shape[::-1], jnp.float32),
            pltpu.SemaphoreType.DMA((2,)),
        ],
        compiler_params=small,
        name="weights",
    )(lengths, hbm(expert_ids.T), hbm(gate_probs.T))
    sent = after(tokens, own_w)
    s1 = over_ring(sent, 1)
    y_w = over_y(own_w)
    y_own = over_y(after(tokens, y_w))
    columns = pl.pallas_call(
        column_kernel,
        in_specs=[vmem] * 4,
        out_specs=[vmem] * ring,
        out_shape=[jax.ShapeDtypeStruct((8, lanes), jnp.float32)] * ring,
        compiler_params=small,
        name="columns",
    )(own_w, y_w, over_core(own_w), over_core(y_w))
    columns = [over_ring(column, k) for k, column in enumerate(columns)]
    s1 = after(s1, y_own, *columns[1:])
    s2 = over_ring(s1, 1)
    s3 = over_ring(s2, 1)
    y1, y2, y3 = over_y(s1), over_y(s2), over_y(s3)
    weight = pl.pallas_call(
        functools.partial(rank_kernel, spare_blocks),
        in_specs=[smem, smem] + [vmem] * ring,
        out_specs=vmem,
        out_shape=jax.ShapeDtypeStruct((devices, lanes), jnp.float32),
        scratch_shapes=[pltpu.VMEM((devices, lanes), jnp.float32)],
        compiler_params=small,
        name="ranks",
    )(block_counts, hot_list.T, *columns)

    def expert(k, *pieces):
        return expert_rows(k, pieces, weight, matrices)

    def merge_core(a, b, cd):
        cd = over_core(cd)
        return f32(a) + f32(cd[:tok_rows]), bf16(f32(b) + f32(cd[tok_rows:]))

    y1 = after(y1, matrices[0], weight)
    p1 = expert(1, after(s1, s2), y1, over_core(s1), over_core(y1))
    y2 = after(y2, p1[0])
    p2 = expert(2, after(s2, s3), y2, over_core(s2), over_core(y2))
    y3 = after(y3, p2[0])
    a2, b2 = merge_core(p2[0], p2[1], after(p2[2], y3))
    p3 = expert(3, after(s3, b2), y3, over_core(s3), over_core(y3))

    (a1, b1), (a3, b3) = map(lambda p: merge_core(*p), (p1, p3))
    block2 = bf16(a2 + f32(after(over_y(b2), p3[0])))
    hop = over_ring(block2, ring - 1)
    own, y_own = after(tokens, b2), after(y_own, b2)
    p0 = expert(0, after(own, block2, b3), y_own, over_core(own), over_core(y_own))
    a0, b0 = merge_core(*p0)
    block1 = a1 + f32(after(over_y(after(b1, b2)), block2, b3, p0[0]))
    block3 = bf16(a3 + f32(over_y(b3)))
    hop = over_ring(bf16(block1 + f32(hop)), ring - 1)
    block0 = a0 + f32(over_y(after(b0, b3)))
    return bf16(block0 + f32(over_ring(block3, 1)) + f32(hop))


def per_device(tokens, expert_ids, gate_probs, lengths, block_counts, hot_list, *weights):
    devices = lax.axis_size("ep")
    slot_rows = plan_sizes(devices, tokens.shape[0], expert_ids.shape[1], hot_list.shape[0])[0]
    layer = dense_layer if slot_rows == tokens.shape[0] and devices == 16 else sparse_layer
    return layer(tokens, expert_ids, gate_probs, lengths, block_counts, hot_list, *weights)


def solution(mesh):
    placed = (
        P(("parts", "ep"), None),
        P(("parts", "ep"), None),
        P(("parts", "ep"), None),
        P(("parts", "ep")),
        P("parts"),
        P("parts", None),
        P("ep", None, None),
        P("ep", None, None),
        P("ep", None, None),
    )
    return jax.shard_map(
        per_device, mesh=mesh, in_specs=placed, out_specs=P(("parts", "ep"), None), check_vma=False
    )
```

```python
import functools

import jax
import jax.numpy as jnp
from jax import lax
from jax.experimental import pallas as pl
from jax.experimental.pallas import tpu as pltpu
from jax.sharding import PartitionSpec as P

BLOCK_LEN = 32
BLK = 128


def expert_forward(gathered, w_gate_e, w_up_e, w_down_e):
    gate = jnp.dot(gathered, w_gate_e, preferred_element_type=jnp.float32)
    up_val = jnp.dot(gathered, w_up_e, preferred_element_type=jnp.float32)
    activation = (jax.nn.silu(gate) * up_val).astype(jnp.bfloat16)
    return jnp.dot(activation, w_down_e, preferred_element_type=jnp.float32).astype(jnp.bfloat16)


def plan_sizes(devices, tok_rows, fan_out, listed):
    assigned = tok_rows * fan_out
    slot_rows = min(2 * assigned // devices, tok_rows)
    cold_load = 3 * devices * (assigned - listed * slot_rows) // (4 * (devices - listed))
    own_blocks = (cold_load + BLK - 1) // BLK
    hot_load = 3 * devices * slot_rows // 4
    spare_blocks = ((hot_load + BLK - 1) // BLK - own_blocks) // 2
    return (slot_rows, own_blocks + spare_blocks, spare_blocks)


def run_blocks(buffer, gate_w, up_w, down_w):
    return expert_forward(buffer, gate_w, up_w, down_w)


def sparse_layer(
    tokens, expert_ids, gate_probs, lengths, block_counts, hot_list, w_gate, w_up, w_down
):
    devices = lax.axis_size("ep")
    my_index = lax.axis_index("ep")
    tok_rows, model_width = tokens.shape
    fan_out = expert_ids.shape[1]
    assigned = tok_rows * fan_out
    slot_rows, most_blocks, spare_blocks = plan_sizes(devices, tok_rows, fan_out, hot_list.shape[0])
    position = jnp.arange(tok_rows, dtype=jnp.int32)
    is_valid = position % BLOCK_LEN < jnp.repeat(lengths, BLOCK_LEN)
    flat_ids = expert_ids.reshape(assigned)
    flat_valid = jnp.repeat(is_valid, fan_out)
    experts = jnp.arange(devices, dtype=jnp.int32)
    onehot = ((flat_ids[:, None] == experts[None, :]) & flat_valid[:, None]).astype(jnp.int32)
    local_rank = jnp.sum((jnp.cumsum(onehot, axis=0) - onehot) * onehot, axis=1)
    counts = jnp.sum(onehot, axis=0)
    all_counts = lax.all_gather(counts[None, :], "ep", axis=0, tiled=True)
    prefix = jnp.cumsum(all_counts, axis=0) - all_counts
    is_hot = jnp.sum((hot_list[:, 0][None, :] == experts[:, None]).astype(jnp.int32), axis=1)
    own_cap = BLK * block_counts
    spare_cap = spare_blocks * BLK * is_hot
    slot_place = jnp.where(flat_valid, flat_ids * slot_rows + local_rank, devices * slot_rows)
    slot_table = jnp.full((devices * slot_rows,), assigned, jnp.int32)
    slot_table = slot_table.at[slot_place].set(jnp.arange(assigned, dtype=jnp.int32), mode="drop")
    padded = jnp.concatenate([tokens, jnp.zeros((1, model_width), tokens.dtype)], axis=0)
    outgoing = padded[slot_table // fan_out].reshape(devices, slot_rows, model_width)
    incoming = lax.all_to_all(outgoing, "ep", split_axis=0, concat_axis=0, tiled=True).reshape(
        devices * slot_rows, model_width
    )
    incoming_pad = jnp.concatenate([incoming, jnp.zeros((1, model_width), incoming.dtype)], axis=0)
    all_slots = devices * slot_rows
    from_counts = lax.dynamic_index_in_dim(all_counts, my_index, 1, keepdims=False)
    from_prefix = lax.dynamic_index_in_dim(prefix, my_index, 1, keepdims=False)
    slot_index = jnp.arange(slot_rows, dtype=jnp.int32)
    global_rank = (from_prefix[:, None] + slot_index[None, :]).reshape(all_slots)
    is_live = (slot_index[None, :] < from_counts[:, None]).reshape(all_slots)
    my_own = lax.dynamic_index_in_dim(own_cap, my_index, 0, keepdims=False)
    my_spare = lax.dynamic_index_in_dim(spare_cap, my_index, 0, keepdims=False)
    rank_limit = my_own + my_spare
    buffer_rows = (most_blocks + spare_blocks) * BLK
    inside = is_live & (global_rank >= 0) & (global_rank < 0 + rank_limit)
    where_to = jnp.where(inside, global_rank - 0, buffer_rows)
    rank_order = jnp.full((buffer_rows,), all_slots, jnp.int32)
    rank_order = rank_order.at[where_to].set(jnp.arange(all_slots, dtype=jnp.int32), mode="drop")
    rows_all = incoming_pad[rank_order]
    results = run_blocks(rows_all, w_gate[0], w_up[0], w_down[0])
    is_kept = is_live & (global_rank < rank_limit)
    result_rows = results.shape[0]
    results_pad = jnp.concatenate([results, jnp.zeros((1, model_width), results.dtype)], axis=0)
    returning = results_pad[jnp.where(is_kept, global_rank, result_rows)].reshape(
        devices, slot_rows, model_width
    )
    returned = lax.all_to_all(returning, "ep", split_axis=0, concat_axis=0, tiled=True).reshape(
        all_slots, model_width
    )
    returned_pad = jnp.concatenate([returned, jnp.zeros((1, model_width), returned.dtype)], axis=0)
    picked = returned_pad[slot_place].reshape(tok_rows, fan_out, model_width)
    weights = jnp.where(is_valid[:, None], gate_probs, 0.0)
    mixed_sum = jnp.zeros((tok_rows, model_width), jnp.float32)
    for column in range(fan_out):
        mixed_sum = mixed_sum + weights[:, column, None] * picked[:, column, :].astype(jnp.float32)
    return mixed_sum.astype(jnp.bfloat16)


def weight_kernel(lengths_ref, ids_ref, probs_ref, out, lengths, ids, probs, sems):
    copies = [
        pltpu.make_async_copy(ids_ref, ids, sems.at[0]),
        pltpu.make_async_copy(probs_ref, probs, sems.at[1]),
        pltpu.make_async_copy(lengths_ref, lengths, sems.at[2]),
    ]
    for copy in copies:
        copy.start()
    for copy in copies:
        copy.wait()
    fan_out, rows = ids.shape
    experts, lanes = out.shape
    token = lax.broadcasted_iota(jnp.int32, (experts, rows), 1)
    expert = lax.broadcasted_iota(jnp.int32, (experts, rows), 0)
    live_len = jnp.zeros((experts, rows), jnp.int32)
    for block in range(lengths.shape[0]):
        live_len = jnp.where(token // BLOCK_LEN == block, lengths[block], live_len)
    is_valid = token % BLOCK_LEN < live_len
    weight = jnp.full((experts, rows), -1.0, jnp.float32)
    for k in range(fan_out):
        weight = jnp.where(is_valid & (ids[k : k + 1, :] == expert), probs[k : k + 1, :], weight)
    out[...] = jnp.full((experts, lanes), -1.0, jnp.float32)
    out[:, :rows] = weight


def load_kernel(*refs):
    half = len(refs) // 2
    copies = [
        pltpu.make_async_copy(refs[i], refs[half + i], refs[-1].at[i]) for i in range(half)
    ]
    for copy in copies:
        copy.start()
    for copy in copies:
        copy.wait()


def column_kernel(w0, w1, w2, w3, *outs):
    me = lax.axis_index("ep")
    ring = len(outs)
    for k, out in enumerate(outs):
        expert = (me // 4 + k) % ring * 4 + me % 4
        for row, ref in enumerate((w0, w1, w2, w3)):
            out[row : row + 1, :] = ref[pl.ds(expert, 1), :]


def rank_kernel(spare_blocks, block_counts, hot_list, *refs):
    columns, out, held = refs[:-2], refs[-2], refs[-1]
    me = lax.axis_index("ep")
    ring = len(columns)
    slots, lanes = out.shape
    for k, ref in enumerate(columns):
        held[4 * k : 4 * k + 4, :] = ref[:4, :]
    weight = held[...]
    live = weight >= 0.0
    ones = live.astype(jnp.float32)
    first = lax.broadcasted_iota(jnp.int32, (lanes, lanes), 0)
    second = lax.broadcasted_iota(jnp.int32, (lanes, lanes), 1)
    earlier = (first < second).astype(jnp.bfloat16)
    rank = jnp.dot(ones.astype(jnp.bfloat16), earlier, preferred_element_type=jnp.float32)
    counts = jnp.sum(ones, axis=1, keepdims=True)

    def source(slot):
        k, core, y = slot // 4, slot // 2 % 2, slot % 2
        return (me // 4 - k + ring) % ring * 4 + (me // 2 + y) % 2 * 2 + (me + core) % 2

    place = source(lax.broadcasted_iota(jnp.int32, (slots, 1), 0))
    before = jnp.zeros((slots, 1), jnp.float32)
    for slot in range(slots):
        before = before + jnp.where(source(slot) < place, counts[slot : slot + 1, :], 0.0)
    limit = block_counts[me]
    for row in range(hot_list.shape[1]):
        limit = limit + jnp.where(hot_list[0, row] == me, spare_blocks, 0)
    kept = live & (rank + before < (limit * BLK).astype(jnp.float32))
    out[...] = jnp.where(kept, weight, 0.0)


def expert_kernel(slot, a, b, c, d, weight, w_gate, w_up, w_down, o_a, o_b, o_cd, *scratch):
    x, act, res, in_sem, out_sem = scratch
    rows, width = a.shape
    hidden = act.shape[1]
    tile, out_tile = min(256, hidden), width // (out_sem.shape[0] // 3)
    copies = [
        pltpu.make_async_copy(src, x.at[pl.ds(i * rows, rows)], in_sem.at[i])
        for i, src in enumerate((a, b, c, d))
    ]
    for copy in copies:
        copy.start()
    row = lax.broadcasted_iota(jnp.int32, (rows, weight.shape[1]), 0)
    lane = lax.broadcasted_iota(jnp.int32, (rows, weight.shape[1]), 1)
    scale = jnp.concatenate(
        [
            jnp.sum(jnp.where(row == lane, weight[4 * slot + i : 4 * slot + i + 1, :], 0.0), axis=1, keepdims=True)
            for i in range(4)
        ],
        axis=0,
    )
    for copy in copies:
        copy.wait()
    for j in range(hidden // tile):
        part = slice(j * tile, (j + 1) * tile)
        gate = jnp.dot(x[...], w_gate[:, part], preferred_element_type=jnp.float32)
        up_val = jnp.dot(x[...], w_up[:, part], preferred_element_type=jnp.float32)
        act[:, part] = (gate / (1.0 + jnp.exp(-gate)) * up_val).astype(act.dtype)
    sent = []
    for j in range(width // out_tile):
        part = slice(j * out_tile, (j + 1) * out_tile)
        result = jnp.dot(act[...], w_down[:, part], preferred_element_type=jnp.float32)
        res[:, part] = (result * scale).astype(res.dtype)
        at = pl.ds(j * out_tile, out_tile)
        for i, (out, start) in enumerate(((o_cd, 2), (o_b, 1), (o_a, 0))):
            src = res.at[pl.ds(start * rows, out.shape[0]), at]
            sent.append(pltpu.make_async_copy(src, out.at[:, at], out_sem.at[3 * j + i]))
            sent[-1].start()
    for copy in sent:
        copy.wait()


def expert_rows(slot, pieces, weight, matrices):
    rows, width = pieces[0].shape
    hidden = matrices[0].shape[1]
    dtype = pieces[0].dtype
    anywhere = pl.BlockSpec(memory_space=pl.ANY)
    vmem = pl.BlockSpec(memory_space=pltpu.VMEM)
    out_steps = 4
    matrices = [pltpu.with_memory_space_constraint(m, pltpu.VMEM) for m in matrices]
    return pl.pallas_call(
        functools.partial(expert_kernel, slot),
        in_specs=[anywhere] * 4 + [vmem] * 4,
        out_specs=[anywhere] * 3,
        out_shape=[
            jax.ShapeDtypeStruct((rows, width), dtype),
            jax.ShapeDtypeStruct((rows, width), dtype),
            jax.ShapeDtypeStruct((2 * rows, width), dtype),
        ],
        scratch_shapes=[
            pltpu.VMEM((4 * rows, width), dtype),
            pltpu.VMEM((4 * rows, hidden), dtype),
            pltpu.VMEM((4 * rows, width), dtype),
            pltpu.SemaphoreType.DMA((4,)),
            pltpu.SemaphoreType.DMA((3 * out_steps,)),
        ],
        compiler_params=pltpu.CompilerParams(vmem_limit_bytes=20 * 1024 * 1024),
        cost_estimate=pl.CostEstimate(
            flops=24 * rows * width * hidden,
            bytes_accessed=6 * width * hidden + 16 * rows * width,
            transcendentals=4 * rows * hidden,
        ),
        name="expert",
    )(*pieces, weight, *matrices)


def dense_layer(
    tokens, expert_ids, gate_probs, lengths, block_counts, hot_list, w_gate, w_up, w_down
):
    devices = lax.axis_size("ep")
    ring = devices // 4
    tok_rows = tokens.shape[0]
    lanes = (tok_rows + 127) // 128 * 128
    spare_blocks = plan_sizes(devices, tok_rows, expert_ids.shape[1], hot_list.shape[0])[2]

    def ring_pairs(k):
        return [(d, (d + 4 * k) % devices) for d in range(devices)]

    core_pairs = [(d, d ^ 1) for d in range(devices)]
    y_pairs = [(d, d ^ 2) for d in range(devices)]
    over_ring = lambda a, k: lax.ppermute(a, "ep", ring_pairs(k)) if k else a
    over_y = lambda a: lax.ppermute(a, "ep", y_pairs)
    over_core = lambda a: lax.ppermute(a, "ep", core_pairs)
    after = lambda value, *others: lax.optimization_barrier((value,) + others)[0]
    f32 = lambda v: v.astype(jnp.float32)
    bf16 = lambda v: v.astype(jnp.bfloat16)
    vmem = pl.BlockSpec(memory_space=pltpu.VMEM)
    smem = pl.BlockSpec(memory_space=pltpu.SMEM)
    anywhere = pl.BlockSpec(memory_space=pl.ANY)
    hbm = lambda v: pltpu.with_memory_space_constraint(v, pltpu.HBM)
    small = pltpu.CompilerParams(vmem_limit_bytes=2 * 1024 * 1024)

    matrices = [hbm(m[0]) for m in (w_gate, w_up, w_down)]
    matrices = pl.pallas_call(
        load_kernel,
        in_specs=[anywhere] * 3,
        out_specs=[vmem] * 3,
        out_shape=[pltpu.VMEM(m.shape, m.dtype) for m in matrices],
        scratch_shapes=[pltpu.SemaphoreType.DMA((3,))],
        compiler_params=small,
        name="load",
    )(*matrices)
    own_w = pl.pallas_call(
        weight_kernel,
        in_specs=[anywhere] * 3,
        out_specs=vmem,
        out_shape=jax.ShapeDtypeStruct((devices, lanes), jnp.float32),
        scratch_shapes=[
            pltpu.SMEM(lengths.shape, jnp.int32),
            pltpu.VMEM(expert_ids.shape[::-1], jnp.int32),
            pltpu.VMEM(gate_probs.shape[::-1], jnp.float32),
            pltpu.SemaphoreType.DMA((3,)),
        ],
        compiler_params=small,
        name="weights",
    )(hbm(lengths), hbm(expert_ids.T), hbm(gate_probs.T))
    sent = after(tokens, own_w)
    s1 = over_ring(sent, 1)
    y_w = over_y(own_w)
    y_own = over_y(after(tokens, y_w))
    columns = pl.pallas_call(
        column_kernel,
        in_specs=[vmem] * 4,
        out_specs=[vmem] * ring,
        out_shape=[jax.ShapeDtypeStruct((8, lanes), jnp.float32)] * ring,
        compiler_params=small,
        name="columns",
    )(own_w, y_w, over_core(own_w), over_core(y_w))
    columns = [over_ring(column, k) for k, column in enumerate(columns)]
    s1 = after(s1, y_own, *columns[1:])
    s2 = over_ring(s1, 1)
    s3 = over_ring(s2, 1)
    y1, y2, y3 = over_y(s1), over_y(s2), over_y(s3)
    weight = pl.pallas_call(
        functools.partial(rank_kernel, spare_blocks),
        in_specs=[smem, smem] + [vmem] * ring,
        out_specs=vmem,
        out_shape=jax.ShapeDtypeStruct((devices, lanes), jnp.float32),
        scratch_shapes=[pltpu.VMEM((devices, lanes), jnp.float32)],
        compiler_params=small,
        name="ranks",
    )(block_counts, hot_list.T, *columns)

    def expert(k, *pieces):
        return expert_rows(k, pieces, weight, matrices)

    def merge_core(a, b, cd):
        cd = over_core(cd)
        return f32(a) + f32(cd[:tok_rows]), bf16(f32(b) + f32(cd[tok_rows:]))

    y1 = after(y1, matrices[0], weight)
    p1 = expert(1, after(s1, s2), y1, over_core(s1), over_core(y1))
    y2 = after(y2, p1[0])
    p2 = expert(2, after(s2, s3), y2, over_core(s2), over_core(y2))
    y3 = after(y3, p2[0])
    a2, b2 = merge_core(p2[0], p2[1], after(p2[2], y3))
    p3 = expert(3, after(s3, b2), y3, over_core(s3), over_core(y3))

    (a1, b1), (a3, b3) = map(lambda p: merge_core(*p), (p1, p3))
    block2 = bf16(a2 + f32(after(over_y(b2), p3[0])))
    hop = over_ring(block2, ring - 1)
    own, y_own = after(tokens, b2), after(y_own, b2)
    p0 = expert(0, after(own, block2, b3), y_own, over_core(own), over_core(y_own))
    a0, b0 = merge_core(*p0)
    block1 = a1 + f32(after(over_y(after(b1, b2)), block2, b3, p0[0]))
    block3 = bf16(a3 + f32(over_y(b3)))
    hop = over_ring(bf16(block1 + f32(hop)), ring - 1)
    block0 = a0 + f32(over_y(after(b0, b3)))
    return bf16(block0 + f32(over_ring(block3, 1)) + f32(hop))


def per_device(tokens, expert_ids, gate_probs, lengths, block_counts, hot_list, *weights):
    devices = lax.axis_size("ep")
    slot_rows = plan_sizes(devices, tokens.shape[0], expert_ids.shape[1], hot_list.shape[0])[0]
    layer = dense_layer if slot_rows == tokens.shape[0] and devices == 16 else sparse_layer
    return layer(tokens, expert_ids, gate_probs, lengths, block_counts, hot_list, *weights)


def solution(mesh):
    placed = (
        P(("parts", "ep"), None),
        P(("parts", "ep"), None),
        P(("parts", "ep"), None),
        P(("parts", "ep")),
        P("parts"),
        P("parts", None),
        P("ep", None, None),
        P("ep", None, None),
        P("ep", None, None),
    )
    return jax.shard_map(
        per_device, mesh=mesh, in_specs=placed, out_specs=P(("parts", "ep"), None), check_vma=False
    )
```

```python
import functools

import jax
import jax.numpy as jnp
from jax import lax
from jax.experimental import pallas as pl
from jax.experimental.pallas import tpu as pltpu
from jax.sharding import PartitionSpec as P

BLOCK_LEN = 32
BLK = 128


def expert_forward(gathered, w_gate_e, w_up_e, w_down_e):
    gate = jnp.dot(gathered, w_gate_e, preferred_element_type=jnp.float32)
    up_val = jnp.dot(gathered, w_up_e, preferred_element_type=jnp.float32)
    activation = (jax.nn.silu(gate) * up_val).astype(jnp.bfloat16)
    return jnp.dot(activation, w_down_e, preferred_element_type=jnp.float32).astype(jnp.bfloat16)


def plan_sizes(devices, tok_rows, fan_out, listed):
    assigned = tok_rows * fan_out
    slot_rows = min(2 * assigned // devices, tok_rows)
    cold_load = 3 * devices * (assigned - listed * slot_rows) // (4 * (devices - listed))
    own_blocks = (cold_load + BLK - 1) // BLK
    hot_load = 3 * devices * slot_rows // 4
    spare_blocks = ((hot_load + BLK - 1) // BLK - own_blocks) // 2
    return (slot_rows, own_blocks + spare_blocks, spare_blocks)


def run_blocks(buffer, gate_w, up_w, down_w):
    return expert_forward(buffer, gate_w, up_w, down_w)


def sparse_layer(
    tokens, expert_ids, gate_probs, lengths, block_counts, hot_list, w_gate, w_up, w_down
):
    devices = lax.axis_size("ep")
    my_index = lax.axis_index("ep")
    tok_rows, model_width = tokens.shape
    fan_out = expert_ids.shape[1]
    assigned = tok_rows * fan_out
    slot_rows, most_blocks, spare_blocks = plan_sizes(devices, tok_rows, fan_out, hot_list.shape[0])
    position = jnp.arange(tok_rows, dtype=jnp.int32)
    is_valid = position % BLOCK_LEN < jnp.repeat(lengths, BLOCK_LEN)
    flat_ids = expert_ids.reshape(assigned)
    flat_valid = jnp.repeat(is_valid, fan_out)
    experts = jnp.arange(devices, dtype=jnp.int32)
    onehot = ((flat_ids[:, None] == experts[None, :]) & flat_valid[:, None]).astype(jnp.int32)
    local_rank = jnp.sum((jnp.cumsum(onehot, axis=0) - onehot) * onehot, axis=1)
    counts = jnp.sum(onehot, axis=0)
    all_counts = lax.all_gather(counts[None, :], "ep", axis=0, tiled=True)
    prefix = jnp.cumsum(all_counts, axis=0) - all_counts
    is_hot = jnp.sum((hot_list[:, 0][None, :] == experts[:, None]).astype(jnp.int32), axis=1)
    own_cap = BLK * block_counts
    spare_cap = spare_blocks * BLK * is_hot
    slot_place = jnp.where(flat_valid, flat_ids * slot_rows + local_rank, devices * slot_rows)
    slot_table = jnp.full((devices * slot_rows,), assigned, jnp.int32)
    slot_table = slot_table.at[slot_place].set(jnp.arange(assigned, dtype=jnp.int32), mode="drop")
    padded = jnp.concatenate([tokens, jnp.zeros((1, model_width), tokens.dtype)], axis=0)
    outgoing = padded[slot_table // fan_out].reshape(devices, slot_rows, model_width)
    incoming = lax.all_to_all(outgoing, "ep", split_axis=0, concat_axis=0, tiled=True).reshape(
        devices * slot_rows, model_width
    )
    incoming_pad = jnp.concatenate([incoming, jnp.zeros((1, model_width), incoming.dtype)], axis=0)
    all_slots = devices * slot_rows
    from_counts = lax.dynamic_index_in_dim(all_counts, my_index, 1, keepdims=False)
    from_prefix = lax.dynamic_index_in_dim(prefix, my_index, 1, keepdims=False)
    slot_index = jnp.arange(slot_rows, dtype=jnp.int32)
    global_rank = (from_prefix[:, None] + slot_index[None, :]).reshape(all_slots)
    is_live = (slot_index[None, :] < from_counts[:, None]).reshape(all_slots)
    my_own = lax.dynamic_index_in_dim(own_cap, my_index, 0, keepdims=False)
    my_spare = lax.dynamic_index_in_dim(spare_cap, my_index, 0, keepdims=False)
    rank_limit = my_own + my_spare
    buffer_rows = (most_blocks + spare_blocks) * BLK
    inside = is_live & (global_rank >= 0) & (global_rank < 0 + rank_limit)
    where_to = jnp.where(inside, global_rank - 0, buffer_rows)
    rank_order = jnp.full((buffer_rows,), all_slots, jnp.int32)
    rank_order = rank_order.at[where_to].set(jnp.arange(all_slots, dtype=jnp.int32), mode="drop")
    rows_all = incoming_pad[rank_order]
    results = run_blocks(rows_all, w_gate[0], w_up[0], w_down[0])
    is_kept = is_live & (global_rank < rank_limit)
    result_rows = results.shape[0]
    results_pad = jnp.concatenate([results, jnp.zeros((1, model_width), results.dtype)], axis=0)
    returning = results_pad[jnp.where(is_kept, global_rank, result_rows)].reshape(
        devices, slot_rows, model_width
    )
    returned = lax.all_to_all(returning, "ep", split_axis=0, concat_axis=0, tiled=True).reshape(
        all_slots, model_width
    )
    returned_pad = jnp.concatenate([returned, jnp.zeros((1, model_width), returned.dtype)], axis=0)
    picked = returned_pad[slot_place].reshape(tok_rows, fan_out, model_width)
    weights = jnp.where(is_valid[:, None], gate_probs, 0.0)
    mixed_sum = jnp.zeros((tok_rows, model_width), jnp.float32)
    for column in range(fan_out):
        mixed_sum = mixed_sum + weights[:, column, None] * picked[:, column, :].astype(jnp.float32)
    return mixed_sum.astype(jnp.bfloat16)


def weight_kernel(lengths_ref, ids_ref, probs_ref, out, lengths, ids, probs, sems):
    copies = [
        pltpu.make_async_copy(ids_ref, ids, sems.at[0]),
        pltpu.make_async_copy(probs_ref, probs, sems.at[1]),
        pltpu.make_async_copy(lengths_ref, lengths, sems.at[2]),
    ]
    for copy in copies:
        copy.start()
    for copy in copies:
        copy.wait()
    fan_out, rows = ids.shape
    experts, lanes = out.shape
    token = lax.broadcasted_iota(jnp.int32, (experts, rows), 1)
    expert = lax.broadcasted_iota(jnp.int32, (experts, rows), 0)
    live_len = jnp.zeros((experts, rows), jnp.int32)
    for block in range(lengths.shape[0]):
        live_len = jnp.where(token // BLOCK_LEN == block, lengths[block], live_len)
    is_valid = token % BLOCK_LEN < live_len
    weight = jnp.full((experts, rows), -1.0, jnp.float32)
    for k in range(fan_out):
        weight = jnp.where(is_valid & (ids[k : k + 1, :] == expert), probs[k : k + 1, :], weight)
    out[...] = jnp.full((experts, lanes), -1.0, jnp.float32)
    out[:, :rows] = weight


def load_kernel(*refs):
    half = len(refs) // 2
    copies = [
        pltpu.make_async_copy(refs[i], refs[half + i], refs[-1].at[i]) for i in range(half)
    ]
    for copy in copies:
        copy.start()
    for copy in copies:
        copy.wait()


def column_kernel(w0, w1, w2, w3, *outs):
    me = lax.axis_index("ep")
    ring = len(outs)
    for k, out in enumerate(outs):
        expert = (me // 4 + k) % ring * 4 + me % 4
        for row, ref in enumerate((w0, w1, w2, w3)):
            out[row : row + 1, :] = ref[pl.ds(expert, 1), :]


def rank_kernel(spare_blocks, block_counts, hot_list, *refs):
    columns, out, held = refs[:-2], refs[-2], refs[-1]
    me = lax.axis_index("ep")
    ring = len(columns)
    slots, lanes = out.shape
    for k, ref in enumerate(columns):
        held[4 * k : 4 * k + 4, :] = ref[:4, :]
    weight = held[...]
    live = weight >= 0.0
    ones = live.astype(jnp.float32)
    first = lax.broadcasted_iota(jnp.int32, (lanes, lanes), 0)
    second = lax.broadcasted_iota(jnp.int32, (lanes, lanes), 1)
    earlier = (first < second).astype(jnp.bfloat16)
    rank = jnp.dot(ones.astype(jnp.bfloat16), earlier, preferred_element_type=jnp.float32)
    counts = jnp.sum(ones, axis=1, keepdims=True)

    def source(slot):
        k, core, y = slot // 4, slot // 2 % 2, slot % 2
        return (me // 4 - k + ring) % ring * 4 + (me // 2 + y) % 2 * 2 + (me + core) % 2

    place = source(lax.broadcasted_iota(jnp.int32, (slots, 1), 0))
    before = jnp.zeros((slots, 1), jnp.float32)
    for slot in range(slots):
        before = before + jnp.where(source(slot) < place, counts[slot : slot + 1, :], 0.0)
    limit = block_counts[me]
    for row in range(hot_list.shape[1]):
        limit = limit + jnp.where(hot_list[0, row] == me, spare_blocks, 0)
    kept = live & (rank + before < (limit * BLK).astype(jnp.float32))
    out[...] = jnp.where(kept, weight, 0.0)


def expert_kernel(slot, a, b, c, d, weight, w_gate, w_up, w_down, o_a, o_b, o_cd, *scratch):
    x, act, res, in_sem, out_sem = scratch
    rows, width = a.shape
    hidden = act.shape[1]
    tile, out_tile = min(256, hidden), width // (out_sem.shape[0] // 3)
    copies = [
        pltpu.make_async_copy(src, x.at[pl.ds(i * rows, rows)], in_sem.at[i])
        for i, src in enumerate((a, b, c, d))
    ]
    for copy in copies:
        copy.start()
    row = lax.broadcasted_iota(jnp.int32, (rows, weight.shape[1]), 0)
    lane = lax.broadcasted_iota(jnp.int32, (rows, weight.shape[1]), 1)
    scale = jnp.concatenate(
        [
            jnp.sum(jnp.where(row == lane, weight[4 * slot + i : 4 * slot + i + 1, :], 0.0), axis=1, keepdims=True)
            for i in range(4)
        ],
        axis=0,
    )
    for copy in copies:
        copy.wait()
    for j in range(hidden // tile):
        part = slice(j * tile, (j + 1) * tile)
        gate = jnp.dot(x[...], w_gate[:, part], preferred_element_type=jnp.float32)
        up_val = jnp.dot(x[...], w_up[:, part], preferred_element_type=jnp.float32)
        act[:, part] = (gate / (1.0 + jnp.exp(-gate)) * up_val).astype(act.dtype)
    sent = []
    for j in range(width // out_tile):
        part = slice(j * out_tile, (j + 1) * out_tile)
        result = jnp.dot(act[...], w_down[:, part], preferred_element_type=jnp.float32)
        res[:, part] = (result * scale).astype(res.dtype)
        at = pl.ds(j * out_tile, out_tile)
        for i, (out, start) in enumerate(((o_cd, 2), (o_b, 1), (o_a, 0))):
            src = res.at[pl.ds(start * rows, out.shape[0]), at]
            sent.append(pltpu.make_async_copy(src, out.at[:, at], out_sem.at[3 * j + i]))
            sent[-1].start()
    for copy in sent:
        copy.wait()


def expert_rows(slot, pieces, weight, matrices):
    rows, width = pieces[0].shape
    hidden = matrices[0].shape[1]
    dtype = pieces[0].dtype
    anywhere = pl.BlockSpec(memory_space=pl.ANY)
    vmem = pl.BlockSpec(memory_space=pltpu.VMEM)
    out_steps = 4
    matrices = [pltpu.with_memory_space_constraint(m, pltpu.VMEM) for m in matrices]
    return pl.pallas_call(
        functools.partial(expert_kernel, slot),
        in_specs=[anywhere] * 4 + [vmem] * 4,
        out_specs=[anywhere] * 3,
        out_shape=[
            jax.ShapeDtypeStruct((rows, width), dtype),
            jax.ShapeDtypeStruct((rows, width), dtype),
            jax.ShapeDtypeStruct((2 * rows, width), dtype),
        ],
        scratch_shapes=[
            pltpu.VMEM((4 * rows, width), dtype),
            pltpu.VMEM((4 * rows, hidden), dtype),
            pltpu.VMEM((4 * rows, width), dtype),
            pltpu.SemaphoreType.DMA((4,)),
            pltpu.SemaphoreType.DMA((3 * out_steps,)),
        ],
        compiler_params=pltpu.CompilerParams(vmem_limit_bytes=20 * 1024 * 1024),
        cost_estimate=pl.CostEstimate(
            flops=24 * rows * width * hidden,
            bytes_accessed=6 * width * hidden + 16 * rows * width,
            transcendentals=4 * rows * hidden,
        ),
        name="expert",
    )(*pieces, weight, *matrices)


def dense_layer(
    tokens, expert_ids, gate_probs, lengths, block_counts, hot_list, w_gate, w_up, w_down
):
    devices = lax.axis_size("ep")
    ring = devices // 4
    tok_rows = tokens.shape[0]
    lanes = (tok_rows + 127) // 128 * 128
    spare_blocks = plan_sizes(devices, tok_rows, expert_ids.shape[1], hot_list.shape[0])[2]

    def ring_pairs(k):
        return [(d, (d + 4 * k) % devices) for d in range(devices)]

    core_pairs = [(d, d ^ 1) for d in range(devices)]
    y_pairs = [(d, d ^ 2) for d in range(devices)]
    over_ring = lambda a, k: lax.ppermute(a, "ep", ring_pairs(k)) if k else a
    over_y = lambda a: lax.ppermute(a, "ep", y_pairs)
    over_core = lambda a: lax.ppermute(a, "ep", core_pairs)
    after = lambda value, *others: lax.optimization_barrier((value,) + others)[0]
    f32 = lambda v: v.astype(jnp.float32)
    bf16 = lambda v: v.astype(jnp.bfloat16)
    vmem = pl.BlockSpec(memory_space=pltpu.VMEM)
    smem = pl.BlockSpec(memory_space=pltpu.SMEM)
    anywhere = pl.BlockSpec(memory_space=pl.ANY)
    hbm = lambda v: pltpu.with_memory_space_constraint(v, pltpu.HBM)
    small = pltpu.CompilerParams(vmem_limit_bytes=2 * 1024 * 1024)

    matrices = [hbm(m[0]) for m in (w_gate, w_up, w_down)]
    matrices = pl.pallas_call(
        load_kernel,
        in_specs=[anywhere] * 3,
        out_specs=[vmem] * 3,
        out_shape=[pltpu.VMEM(m.shape, m.dtype) for m in matrices],
        scratch_shapes=[pltpu.SemaphoreType.DMA((3,))],
        compiler_params=small,
        name="load",
    )(*matrices)
    own_w = pl.pallas_call(
        weight_kernel,
        in_specs=[anywhere] * 3,
        out_specs=vmem,
        out_shape=jax.ShapeDtypeStruct((devices, lanes), jnp.float32),
        scratch_shapes=[
            pltpu.SMEM(lengths.shape, jnp.int32),
            pltpu.VMEM(expert_ids.shape[::-1], jnp.int32),
            pltpu.VMEM(gate_probs.shape[::-1], jnp.float32),
            pltpu.SemaphoreType.DMA((3,)),
        ],
        compiler_params=small,
        name="weights",
    )(hbm(lengths), hbm(expert_ids.T), hbm(gate_probs.T))
    sent = after(tokens, own_w)
    s1 = over_ring(sent, 1)
    y_w = over_y(own_w)
    y_own = over_y(after(tokens, y_w))
    columns = pl.pallas_call(
        column_kernel,
        in_specs=[vmem] * 4,
        out_specs=[vmem] * ring,
        out_shape=[jax.ShapeDtypeStruct((8, lanes), jnp.float32)] * ring,
        compiler_params=small,
        name="columns",
    )(own_w, y_w, over_core(own_w), over_core(y_w))
    columns = [over_ring(column, k) for k, column in enumerate(columns)]
    s1 = after(s1, y_own, *columns[1:])
    s2 = over_ring(s1, 1)
    s3 = over_ring(s2, 1)
    y1, y2, y3 = over_y(s1), over_y(s2), over_y(s3)
    weight = pl.pallas_call(
        functools.partial(rank_kernel, spare_blocks),
        in_specs=[smem, smem] + [vmem] * ring,
        out_specs=vmem,
        out_shape=jax.ShapeDtypeStruct((devices, lanes), jnp.float32),
        scratch_shapes=[pltpu.VMEM((devices, lanes), jnp.float32)],
        compiler_params=small,
        name="ranks",
    )(block_counts, hot_list.T, *columns)

    def expert(k, *pieces):
        return expert_rows(k, pieces, weight, matrices)

    def merge_core(a, b, cd):
        cd = over_core(cd)
        return f32(a) + f32(cd[:tok_rows]), bf16(f32(b) + f32(cd[tok_rows:]))

    y1 = after(y1, matrices[0], weight)
    p1 = expert(1, after(s1, s2), y1, over_core(s1), over_core(y1))
    y2 = after(y2, p1[0])
    p2 = expert(2, after(s2, s3), y2, over_core(s2), over_core(y2))
    y3 = after(y3, p2[0])
    a2, b2 = merge_core(p2[0], p2[1], after(p2[2], y3))
    p3 = expert(3, after(s3, b2), y3, over_core(s3), over_core(y3))

    (a1, b1), (a3, b3) = map(lambda p: merge_core(*p), (p1, p3))
    half = tok_rows // 32 * 16
    y_b2, y_low = over_y(b2[:half]), after(over_y(b2[half:]), p3[0])
    top = bf16(a2[:half] + f32(after(y_b2, p3[0])))
    hop = over_ring(top, ring - 1)
    block2 = bf16(a2[half:] + f32(after(y_low, top)))
    hop = jnp.concatenate([hop, over_ring(block2, ring - 1)])
    own, y_own = after(tokens, b2), after(y_own, b2)
    p0 = expert(0, after(own, block2, b3), y_own, over_core(own), over_core(y_own))
    a0, b0 = merge_core(*p0)
    block1 = a1 + f32(after(over_y(after(b1, b2)), block2, b3, p0[0]))
    block3 = bf16(a3 + f32(over_y(b3)))
    hop = over_ring(bf16(block1 + f32(hop)), ring - 1)
    block0 = a0 + f32(over_y(after(b0, b3)))
    return bf16(block0 + f32(over_ring(block3, 1)) + f32(hop))


def per_device(tokens, expert_ids, gate_probs, lengths, block_counts, hot_list, *weights):
    devices = lax.axis_size("ep")
    slot_rows = plan_sizes(devices, tokens.shape[0], expert_ids.shape[1], hot_list.shape[0])[0]
    layer = dense_layer if slot_rows == tokens.shape[0] and devices == 16 else sparse_layer
    return layer(tokens, expert_ids, gate_probs, lengths, block_counts, hot_list, *weights)


def solution(mesh):
    placed = (
        P(("parts", "ep"), None),
        P(("parts", "ep"), None),
        P(("parts", "ep"), None),
        P(("parts", "ep")),
        P("parts"),
        P("parts", None),
        P("ep", None, None),
        P("ep", None, None),
        P("ep", None, None),
    )
    return jax.shard_map(
        per_device, mesh=mesh, in_specs=placed, out_specs=P(("parts", "ep"), None), check_vma=False
    )
```
